32 devices in a mesh: seq: 8 (over y, x, core), res: 4 (over z).
Axes of the slice: x: 2, y: 2, z: 4, core: 2. Of those that a mesh axis runs over, the one named last changes fastest.
Arguments:
- states: bfloat16 [256, 128, 768], P('seq', 'res'), may hold values from -6 to 6
- row_query: bfloat16 [768, 768], replicated, as said below
- row_key: bfloat16 [768, 768], replicated
- row_value: bfloat16 [768, 768], replicated, may hold values from -0.21875 to 0.21875
- row_out: bfloat16 [768, 768], replicated, may hold values from -0.21875 to 0.21875
- col_query: bfloat16 [768, 768], replicated, as said below
- col_key: bfloat16 [768, 768], replicated
- col_value: bfloat16 [768, 768], replicated, may hold values from -0.21875 to 0.21875
- col_out: bfloat16 [768, 768], replicated, may hold values from -0.21875 to 0.21875
Outputs:
- updated: bfloat16 [256, 128, 768], P('seq', 'res')
The draws below stay inside these ranges and needn't reach their ends.
Inputs may be any that keep to these rules, and one draw needn't show every extreme that they name: No bound on the size of row_query and row_key entries or of the scores they give is promised. No bound on the size of col_query and col_key entries or of the scores they give is promised.
All inputs are finite; a program needn't handle non-finite values.
Results may differ from the reference program's by a relative error of at most 0.02.
Values may be sent and summed in bfloat16 or wider, within the bound.
No kernel may reach another device: no remote copies, remote signals or barrier semaphores. Data moves between devices by JAX's collectives and lax.ppermute only.
A program may use at most 128 MiB of HBM per device.

```python
import math
import jax
import jax.numpy as jnp
from jax import lax

D = 768
HEADS = 12
ROWS = 256
COLS = 128


def query_pair(key, tag):
    base = jax.random.fold_in(key, tag)
    keys_part = jax.random.normal(jax.random.fold_in(base, 1), (D, D), jnp.float32) * D ** (-0.5)
    query_part = jax.random.normal(jax.random.fold_in(base, 2), (D, D), jnp.float32) * 2.0 * D ** (-0.5)
    return (query_part, keys_part)


def draw_row_query(key, part):
    return query_pair(key, 101)[0].astype(jnp.bfloat16)


def draw_row_key(key, part):
    return query_pair(key, 101)[1].astype(jnp.bfloat16)


def draw_col_query(key, part):
    return query_pair(key, 202)[0].astype(jnp.bfloat16)


def draw_col_key(key, part):
    return query_pair(key, 202)[1].astype(jnp.bfloat16)


def levels(stream_key, shape, pieces, low, top_value):
    def one(axis_at, blocks):
        steps = jax.random.uniform(jax.random.fold_in(jax.random.fold_in(stream_key, 6), axis_at), (blocks,), jnp.float32, low / len(pieces), top_value / len(pieces))
        return jnp.repeat(jnp.exp(steps), shape[axis_at] // blocks).reshape((-1,) + (1,) * (len(shape) - axis_at - 1))

    level = one(*pieces[0])
    for cut in pieces[1:]:
        level = level * one(*cut)
    return level


def centred(own_key, dims, scale, reach, shards=(), kind=jnp.bfloat16):
    entries = jax.random.normal(own_key, dims, jnp.float32) * scale
    if len(shards) > 0:
        entries = levels(own_key, dims, shards, -0.22, 0.18) * entries
    return jnp.clip(entries, min=-reach, max=reach).astype(kind)


def setup_inputs(seed: int = 0) -> dict:
    splits = jax.random.split(jax.random.key(seed), 10)
    states = centred(splits[0], (ROWS, COLS, D), 1.0, 6.0, ((0, 8), (1, 4)))
    row_query = draw_row_query(jax.random.fold_in(splits[9], 71), 0)
    row_key = draw_row_key(jax.random.fold_in(splits[9], 71), 0)
    row_value = centred(splits[3], (D, D), D ** -0.5, 0.21875)
    row_out = centred(splits[4], (D, D), D ** -0.5, 0.21875)
    col_query = draw_col_query(jax.random.fold_in(splits[9], 71), 0)
    col_key = draw_col_key(jax.random.fold_in(splits[9], 71), 0)
    col_value = centred(splits[7], (D, D), D ** -0.5, 0.21875)
    col_out = centred(splits[8], (D, D), D ** -0.5, 0.21875)
    return {"states": states, "row_query": row_query, "row_key": row_key, "row_value": row_value, "row_out": row_out, "col_query": col_query, "col_key": col_key, "col_value": col_value, "col_out": col_out}


def normalize(states):
    values = states.astype(jnp.float32)
    center = values - lax.optimization_barrier(jnp.mean(values, axis=-1, keepdims=True))
    spread = lax.optimization_barrier(jnp.mean(center * center, axis=-1, keepdims=True))
    return (center * lax.rsqrt(spread + 1e-05)).astype(jnp.bfloat16)

def project(inputs, weight):
    flat = inputs.reshape(-1, inputs.shape[-1])
    result = jnp.dot(flat, weight, preferred_element_type=jnp.float32)
    return result.reshape(inputs.shape[:-1] + (weight.shape[1],))

def reference(states, row_query, row_key, row_value, row_out, col_query, col_key, col_value, col_out):
    nrows, ncols = (states.shape[0], states.shape[1])
    head_dim = D // HEADS
    normed = normalize(states)
    q1 = project(normed, row_query).astype(jnp.bfloat16).reshape(nrows, ncols, HEADS, head_dim)
    k1 = project(normed, row_key).astype(jnp.bfloat16).reshape(nrows, ncols, HEADS, head_dim)
    v1 = project(normed, row_value).astype(jnp.bfloat16).reshape(nrows, ncols, HEADS, head_dim)
    tied = jnp.einsum('rihd,rjhd->hij', q1.astype(jnp.float32), k1.astype(jnp.float32))
    tied = tied * (head_dim ** (-0.5) / math.sqrt(nrows))
    prob1 = jax.nn.softmax(tied, axis=-1).astype(jnp.bfloat16)
    o1 = jnp.einsum('hij,rjhd->rihd', prob1.astype(jnp.float32), v1.astype(jnp.float32)).astype(jnp.bfloat16)
    mid = (states.astype(jnp.float32) + project(o1.reshape(nrows, ncols, D), row_out)).astype(jnp.bfloat16)
    normed2 = normalize(mid)
    q2 = project(normed2, col_query).astype(jnp.bfloat16)
    k2 = project(normed2, col_key).astype(jnp.bfloat16)
    v2 = project(normed2, col_value).astype(jnp.bfloat16)
    block = math.gcd(ncols, 8)

    def arrange(field):
        field = field.reshape(nrows, ncols, HEADS, head_dim).transpose(1, 0, 2, 3)
        return field.reshape(ncols // block, block, nrows, HEADS, head_dim)

    def attend(triple):
        qb, kb, vb = triple
        score = jnp.einsum('crhd,cshd->chrs', qb.astype(jnp.float32), kb.astype(jnp.float32)) * head_dim ** (-0.5)
        prob2 = jax.nn.softmax(score, axis=-1).astype(jnp.bfloat16)
        return jnp.einsum('chrs,cshd->crhd', prob2.astype(jnp.float32), vb.astype(jnp.float32)).astype(jnp.bfloat16)
    o2 = lax.map(attend, (arrange(q2), arrange(k2), arrange(v2)))
    o2 = o2.reshape(ncols, nrows, D).transpose(1, 0, 2)
    colupd = project(o2, col_out).astype(jnp.bfloat16)
    colupd = lax.optimization_barrier(colupd)
    return (mid.astype(jnp.float32) + colupd.astype(jnp.float32)).astype(jnp.bfloat16)
```

```python
import functools
import math

import jax
import jax.numpy as jnp
from jax import lax
from jax.experimental import pallas as pl
from jax.experimental.pallas import tpu as pltpu
from jax.sharding import Mesh
from jax.sharding import PartitionSpec as P

HEADS = 12
CORES = 2
CHUNKS = 2
VMEM_BYTES = 56 * 1024 * 1024

BF16 = jnp.bfloat16
F32 = jnp.float32


def normalize(values):
    center = values - jnp.mean(values, axis=-1, keepdims=True)
    spread = jnp.mean(center * center, axis=-1, keepdims=True)
    return (center * lax.rsqrt(spread + 1e-05)).astype(BF16)


def dot(left, right):
    return jnp.dot(left, right, preferred_element_type=F32)


def dot_nt(left, right):
    return lax.dot_general(left, right, (((1,), (1,)), ((), ())), preferred_element_type=F32)


def head_masks(shape, head_dim):
    lane = lax.broadcasted_iota(jnp.int32, shape, len(shape) - 1)
    first = lax.rem(lane, 2 * head_dim) < head_dim
    return first, jnp.logical_not(first)


def permutation(size, source):
    wanted = source(lax.broadcasted_iota(jnp.int32, (size, size), 0))
    return (wanted == lax.broadcasted_iota(jnp.int32, (size, size), 1)).astype(F32).astype(BF16)


def row_scores(core_ref, x_ref, wq_ref, wk_ref, wv_ref, mine_ref, other_ref, v_ref):
    parts, rows, block, width = x_ref.shape
    cols = parts * block
    head_dim = width // HEADS
    pair = 2 * head_dim
    half_pairs = HEADS // 2 // CORES
    piece = block // CHUNKS

    values = x_ref[...].astype(F32)
    values = jnp.concatenate(
        [values[:, row].reshape(cols, width) for row in range(rows)], axis=0
    )
    normed = normalize(values)
    q = dot(normed, wq_ref[...])
    k = dot(normed, wk_ref[...])
    v = dot(normed, wv_ref[...])
    v_ref[...] = v.astype(BF16).reshape(rows, cols, width)
    first, second = head_masks(k.shape, head_dim)
    q = q.astype(BF16)
    k_first = jnp.where(first, k, 0.0).astype(BF16)
    k_second = jnp.where(second, k, 0.0).astype(BF16)

    def beside(field, at):
        lanes = slice(at * pair, (at + 1) * pair)
        return jnp.concatenate(
            [field[row * cols : (row + 1) * cols, lanes] for row in range(rows)], axis=1
        )

    scores = []
    for at in range(HEADS // 2):
        keys = jnp.concatenate([beside(k_first, at), beside(k_second, at)], axis=0)
        score = dot_nt(beside(q, at), keys)
        score = score.reshape(parts, CHUNKS, piece, 2 * cols)
        scores.append(jnp.swapaxes(score, 0, 1).reshape(cols, 2 * cols))

    def put(low_ref, high_ref):
        for at in range(half_pairs):
            low, high = scores[at], scores[half_pairs + at]

            @pl.when(pl.program_id(0) == 0)
            def _():
                low_ref[at] = low
                high_ref[at] = high

            @pl.when(pl.program_id(0) > 0)
            def _():
                low_ref[at] += low
                high_ref[at] += high

    @pl.when(core_ref[0] == 0)
    def _():
        put(mine_ref, other_ref)

    @pl.when(core_ref[0] == 1)
    def _():
        put(other_ref, mine_ref)


def row_softmax(scale, parts_ref, prob_ref):
    tied = parts_ref[0]
    for at in range(1, parts_ref.shape[0]):
        tied = tied + parts_ref[at]
    tied = tied * scale
    cols = tied.shape[1] // 2
    halves = []
    for half in (tied[:, :cols], tied[:, cols:]):
        top = jnp.exp(half - jnp.max(half, axis=-1, keepdims=True))
        halves.append(top / jnp.sum(top, axis=-1, keepdims=True))
    prob = jnp.concatenate(halves, axis=1).astype(BF16)
    for at in range(prob_ref.shape[0]):
        prob_ref[at] = prob


def row_update(seq_size, core_ref, mine_ref, other_ref, v_ref, x_ref, wo_ref, mid_ref, o_ref):
    parts, rows, block, width = x_ref.shape
    cols = parts * block
    head_dim = width // HEADS
    pair = 2 * head_dim
    half_pairs = HEADS // 2 // CORES
    piece = block // CHUNKS
    first, second = head_masks((cols, pair), head_dim)

    for prob_ref, low in ((mine_ref, core_ref[0]), (other_ref, 1 - core_ref[0])):
        for at in range(half_pairs):
            lanes = pl.ds(pl.multiple_of((low * half_pairs + at) * pair, pair), pair)
            prob = prob_ref[at]
            for row in range(0, rows, 2):
                fields = [v_ref[row + step, :, lanes].astype(F32) for step in range(2)]
                values = jnp.concatenate(
                    [
                        jnp.concatenate(
                            [jnp.where(mask, field, 0.0).astype(BF16) for field in fields], axis=1
                        )
                        for mask in (first, second)
                    ],
                    axis=0,
                )
                result = dot(prob, values).astype(BF16)
                o_ref[row, :, lanes] = result[:, :pair]
                o_ref[row + 1, :, lanes] = result[:, pair:]

    tokens = rows * parts * piece
    at_once = piece // seq_size

    def source(token):
        row = lax.rem(token, rows)
        rest = lax.div(token, rows)
        inner = lax.rem(rest, at_once)
        rest = lax.div(rest, at_once)
        part = lax.rem(rest, parts)
        owner = lax.div(rest, parts)
        return (row * parts + part) * piece + owner * at_once + inner

    order = permutation(tokens, source)
    for chunk in range(CHUNKS):
        attended = o_ref[:, chunk * parts * piece : (chunk + 1) * parts * piece, :]
        residual = jnp.swapaxes(x_ref[:, :, chunk * piece : (chunk + 1) * piece, :], 0, 1)
        mid = residual.reshape(tokens, width).astype(F32) + dot(
            attended.reshape(tokens, width), wo_ref[...]
        )
        mid_ref[chunk] = dot(order, mid.astype(BF16)).astype(BF16)


def column_update(at_once, rows, mid_ref, wq_ref, wk_ref, wv_ref, wo_ref, out_ref, o_ref):
    total, width = mid_ref.shape
    all_rows = total // at_once
    head_dim = width // HEADS
    pair = 2 * head_dim
    scale = head_dim ** (-0.5)

    mid = mid_ref[...].astype(F32)
    if at_once > 1:
        mid = mid.reshape(all_rows // rows, at_once, rows, width)
        mid = jnp.concatenate(
            [mid[:, at].reshape(all_rows, width) for at in range(at_once)], axis=0
        )
    normed = normalize(mid)
    q = (dot(normed, wq_ref[...]).astype(BF16) * scale).astype(BF16)
    k = dot(normed, wk_ref[...])
    v = dot(normed, wv_ref[...])
    first, second = head_masks(k.shape, head_dim)
    k_first = jnp.where(first, k, 0.0).astype(BF16)
    k_second = jnp.where(second, k, 0.0).astype(BF16)
    v_first = jnp.where(first, v, 0.0).astype(BF16)
    v_second = jnp.where(second, v, 0.0).astype(BF16)
    one_first, one_second = (
        mask.astype(F32).astype(BF16) for mask in head_masks((all_rows, pair), head_dim)
    )

    for at in range(at_once):
        own = slice(at * all_rows, (at + 1) * all_rows)
        for head in range(HEADS // 2):
            lanes = slice(head * pair, (head + 1) * pair)
            keys = jnp.concatenate([k_first[own, lanes], k_second[own, lanes]], axis=0)
            score = dot_nt(q[own, lanes], keys)
            tops = []
            for half in (score[:, :all_rows], score[:, all_rows:]):
                tops.append(jnp.exp(half - jnp.max(half, axis=-1, keepdims=True)).astype(BF16))
            values = jnp.concatenate(
                [
                    jnp.concatenate([v_first[own, lanes], one_first], axis=1),
                    jnp.concatenate([v_second[own, lanes], one_second], axis=1),
                ],
                axis=0,
            )
            result = dot(jnp.concatenate(tops, axis=1), values)
            o_ref[own, lanes] = (result[:, :pair] / result[:, pair:]).astype(BF16)

    update = dot(o_ref[...], wo_ref[...]).astype(BF16).astype(F32)
    updated = (mid + update).astype(BF16)
    owners, kept = out_ref.shape[0], out_ref.shape[2]
    for at in range(at_once):
        out_ref[:, at] = updated[at * all_rows : (at + 1) * all_rows].reshape(owners, kept, width)


def assemble(*refs):
    out_ref = refs[-1]
    rows, cols, width = out_ref.shape
    pieces = [ref[...].reshape(-1, width) for ref in refs[:-1]]
    tokens = rows * cols

    def source(token):
        return lax.rem(token, cols) * rows + lax.div(token, cols)

    gathered = jnp.concatenate(pieces, axis=0)
    moved = dot(permutation(tokens, source), gathered)
    out_ref[...] = moved.astype(BF16).reshape(rows, cols, width)


def whole(shape):
    return pl.BlockSpec(shape, lambda *_: (0,) * len(shape))


def params():
    return pltpu.CompilerParams(vmem_limit_bytes=VMEM_BYTES)


def cost(flops, moved, special=0):
    return pl.CostEstimate(flops=int(flops), bytes_accessed=int(moved), transcendentals=int(special))


def on_device(
    states, row_query, row_key, row_value, row_out, col_query, col_key, col_value, col_out
):
    rows, block, width = states.shape
    pairs_size, res_size = lax.axis_size("pair"), lax.axis_size("res")
    seq_size = pairs_size * CORES
    all_rows, cols = rows * seq_size, block * res_size
    head_dim = width // HEADS
    own_rows = rows // res_size
    half_pairs = HEADS // 2 // CORES
    core = lax.axis_index("core").astype(jnp.int32).reshape(1)
    swap = [(0, 1), (1, 0)]
    smem = pl.BlockSpec(memory_space=pltpu.SMEM)
    weight = whole((width, width))

    x = lax.all_to_all(states, "res", split_axis=0, concat_axis=0, tiled=True)
    x = x.reshape(res_size, own_rows, block, width)

    at_once = min(2, own_rows)
    tied_shape = (half_pairs, cols, 2 * cols)
    mine, other, v = pl.pallas_call(
        row_scores,
        grid=(own_rows // at_once,),
        in_specs=[smem, pl.BlockSpec((res_size, at_once, block, width), lambda g: (0, g, 0, 0))]
        + [weight] * 3,
        out_specs=[
            whole(tied_shape),
            whole(tied_shape),
            pl.BlockSpec((at_once, cols, width), lambda g: (g, 0, 0)),
        ],
        out_shape=[
            jax.ShapeDtypeStruct(tied_shape, F32),
            jax.ShapeDtypeStruct(tied_shape, F32),
            jax.ShapeDtypeStruct((own_rows, cols, width), BF16),
        ],
        compiler_params=params(),
        cost_estimate=cost(8 * own_rows * cols * width * width, 12e6),
        name="row_scores",
    )(core, x, row_query, row_key, row_value)

    shares = pairs_size * res_size
    partial = mine + lax.ppermute(other, "core", swap)
    partial = partial.reshape(shares, half_pairs * cols // shares, 2 * cols)
    partial = lax.all_to_all(partial, ("pair", "res"), split_axis=0, concat_axis=0, tiled=True)
    prob = pl.pallas_call(
        functools.partial(row_softmax, head_dim ** (-0.5) / math.sqrt(all_rows)),
        out_shape=jax.ShapeDtypeStruct(partial.shape, BF16),
        compiler_params=params(),
        name="row_softmax",
    )(partial)
    prob = lax.all_to_all(prob, ("pair", "res"), split_axis=0, concat_axis=0, tiled=True)
    prob = prob.reshape(tied_shape)
    prob_other = lax.ppermute(prob, "core", swap)

    tokens = own_rows * cols // CHUNKS
    mid = pl.pallas_call(
        functools.partial(row_update, seq_size),
        in_specs=[smem]
        + [pl.BlockSpec(memory_space=pltpu.VMEM)] * 5,
        out_shape=jax.ShapeDtypeStruct((CHUNKS, tokens, width), BF16),
        scratch_shapes=[pltpu.VMEM((own_rows, cols, width), BF16)],
        compiler_params=params(),
        cost_estimate=cost(3 * own_rows * cols * width * width, 8e6),
        name="row_update",
    )(core, prob, prob_other, v, x, row_out)

    col_at_once = block // CHUNKS // seq_size
    out = []
    for chunk in range(CHUNKS):
        moved = lax.all_to_all(
            mid[chunk], ("pair", "core", "res"), split_axis=0, concat_axis=0, tiled=True
        )
        updated = pl.pallas_call(
            functools.partial(column_update, col_at_once, own_rows),
            out_shape=jax.ShapeDtypeStruct((seq_size, col_at_once, rows, width), BF16),
            scratch_shapes=[pltpu.VMEM((tokens, width), BF16)],
            compiler_params=params(),
            cost_estimate=cost(10 * tokens * width * width, 8e6, tokens * all_rows * HEADS),
            name="column_update",
        )(moved, col_query, col_key, col_value, col_out)
        out.append(
            lax.all_to_all(updated, ("pair", "core"), split_axis=0, concat_axis=0, tiled=True)
        )

    row_step = 16
    piece = pl.BlockSpec((seq_size, col_at_once, row_step, width), lambda g: (0, 0, g, 0))
    return pl.pallas_call(
        assemble,
        grid=(rows // row_step,),
        in_specs=[piece] * CHUNKS,
        out_specs=pl.BlockSpec((row_step, block, width), lambda g: (g, 0, 0)),
        out_shape=jax.ShapeDtypeStruct((rows, block, width), BF16),
        compiler_params=params(),
        name="assemble",
    )(*out)


def solution(mesh):
    seq_size, res_size = mesh.devices.shape
    split = Mesh(
        mesh.devices.reshape(seq_size // CORES, CORES, res_size), ("pair", "core", "res")
    )
    placed = P(("pair", "core"), "res", None)
    return jax.shard_map(
        on_device,
        mesh=split,
        in_specs=(placed,) + (P(),) * 8,
        out_specs=placed,
        check_vma=False,
    )
```

```python
import functools
import math

import jax
import jax.numpy as jnp
from jax import lax
from jax.experimental import pallas as pl
from jax.experimental.pallas import tpu as pltpu
from jax.sharding import Mesh
from jax.sharding import PartitionSpec as P

HEADS = 12
CORES = 2
SLOT = 16
VMEM_BYTES = 32 * 1024 * 1024

BF16 = jnp.bfloat16
F32 = jnp.float32


def normalize(values):
    center = values - jnp.mean(values, axis=-1, keepdims=True)
    spread = jnp.mean(center * center, axis=-1, keepdims=True)
    return (center * lax.rsqrt(spread + 1e-05)).astype(BF16)


def dot(left, right):
    return jnp.dot(left, right, preferred_element_type=F32)


def dot_nt(left, right):
    return lax.dot_general(left, right, (((1,), (1,)), ((), ())), preferred_element_type=F32)


def head_masks(width, head_dim):
    lane = lax.broadcasted_iota(jnp.int32, (1, width), 1)
    first = (lax.rem(lane, 2 * head_dim) < head_dim).astype(F32)
    return first.astype(BF16), (1.0 - first).astype(BF16)


def permutation(size, source):
    wanted = source(lax.broadcasted_iota(jnp.int32, (size, size), 0))
    return (wanted == lax.broadcasted_iota(jnp.int32, (size, size), 1)).astype(F32).astype(BF16)


def row_project(at_ref, x_ref, wq_ref, wk_ref, wv_ref, *refs):
    q_ref, k_ref, v_ref, kept_ref = refs[-4:]
    rows, block, width = x_ref.shape
    x = x_ref[...]
    kept_ref[...] = x
    normed = normalize(x.astype(F32).reshape(rows * block, width))
    for weight_ref, ref in ((wq_ref, q_ref), (wk_ref, k_ref), (wv_ref, v_ref)):
        ref[...] = dot(normed, weight_ref[...]).astype(BF16).reshape(rows, block, width)


def row_scores(block, chunks, base_ref, q_ref, k_ref, tied_ref):
    rows, cols, pair = q_ref.shape
    first, second = head_masks(pair, pair // 2)
    q = jnp.concatenate([q_ref[row] for row in range(rows)], axis=1)
    keys = jnp.concatenate(
        [
            jnp.concatenate([k_ref[row] * mask for row in range(rows)], axis=1)
            for mask in (first, second)
        ],
        axis=0,
    )
    score = dot_nt(q, keys).reshape(cols // block, block, 2 * cols)
    at = 0
    pieces = []
    for piece in chunks:
        pieces.append(score[:, at : at + piece].reshape(-1, 2 * cols))
        at += piece
    tied_ref[0] = jnp.concatenate(pieces, axis=0)


def row_softmax(scale, parts_ref, prob_ref):
    tied = parts_ref[0]
    for at in range(1, parts_ref.shape[0]):
        tied = tied + parts_ref[at]
    tied = tied * scale
    cols = tied.shape[1] // 2
    halves = []
    for half in (tied[:, :cols], tied[:, cols:]):
        top = jnp.exp(half - jnp.max(half, axis=-1, keepdims=True))
        halves.append(top / jnp.sum(top, axis=-1, keepdims=True))
    prob = jnp.concatenate(halves, axis=1).astype(BF16)
    for at in range(prob_ref.shape[0]):
        prob_ref[at] = prob


def row_update(seq_size, parts, chunks, core_ref, mine_ref, other_ref, v_ref, x_ref, wo_ref, *refs):
    mid_refs, o_ref = refs[:-1], refs[-1]
    rows, cols, width = x_ref.shape
    head_dim = width // HEADS
    pair = 2 * head_dim
    half_pairs = HEADS // 2 // CORES
    masks = head_masks(pair, head_dim)

    for prob_ref, low in ((mine_ref, core_ref[0]), (other_ref, 1 - core_ref[0])):
        for at in range(half_pairs):
            lanes = pl.ds(pl.multiple_of((low * half_pairs + at) * pair, pair), pair)
            prob = prob_ref[at]
            for row in range(0, rows, 2):
                fields = [v_ref[row + step, :, lanes] for step in range(2)]
                values = jnp.concatenate(
                    [
                        jnp.concatenate([field * mask for field in fields], axis=1)
                        for mask in masks
                    ],
                    axis=0,
                )
                result = dot(prob, values).astype(BF16)
                o_ref[row, :, lanes] = result[:, :pair]
                o_ref[row + 1, :, lanes] = result[:, pair:]

    at = 0
    for piece, mid_ref in zip(chunks, mid_refs, strict=True):
        tokens = rows * parts * piece
        inner = piece // seq_size

        def source(token):
            row = lax.rem(token, rows)
            rest = lax.div(token, rows)
            step = lax.rem(rest, inner)
            rest = lax.div(rest, inner)
            part = lax.rem(rest, parts)
            owner = lax.div(rest, parts)
            return (row * parts + part) * piece + owner * inner + step

        attended = o_ref[:, at * parts : (at + piece) * parts, :].reshape(tokens, width)
        residual = x_ref[...].astype(F32).reshape(rows, parts, cols // parts, width)
        residual = residual[:, :, at : at + piece].reshape(tokens, width)
        mid = residual + dot(attended, wo_ref[...])
        mid_ref[...] = dot(permutation(tokens, source), mid.astype(BF16)).astype(BF16)
        at += piece


def column_update(
    at_once, rows, seq_ref, mid_ref, wq_ref, wk_ref, wv_ref, wo_ref, *refs
):
    out_refs, o_ref, updated_ref = refs[:-2], refs[-2], refs[-1]
    total, width = mid_ref.shape
    all_rows = total // at_once
    head_dim = width // HEADS
    pair = 2 * head_dim
    scale = head_dim ** (-0.5)

    mid = mid_ref[...].astype(F32)
    if at_once > 1:
        mid = mid.reshape(all_rows // rows, at_once, rows, width)
        mid = jnp.concatenate(
            [mid[:, at].reshape(all_rows, width) for at in range(at_once)], axis=0
        )
    normed = normalize(mid)
    q = (dot(normed, wq_ref[...]).astype(BF16) * scale).astype(BF16)
    k = dot(normed, wk_ref[...]).astype(BF16)
    v = dot(normed, wv_ref[...]).astype(BF16)
    masks = head_masks(pair, head_dim)
    ones = [jnp.broadcast_to(mask, (all_rows, pair)) for mask in masks]

    for at in range(at_once):
        own = slice(at * all_rows, (at + 1) * all_rows)
        for head in range(HEADS // 2):
            lanes = slice(head * pair, (head + 1) * pair)
            keys = jnp.concatenate([k[own, lanes] * mask for mask in masks], axis=0)
            score = dot_nt(q[own, lanes], keys)
            tops = []
            for half in (score[:, :all_rows], score[:, all_rows:]):
                tops.append(jnp.exp(half - jnp.max(half, axis=-1, keepdims=True)).astype(BF16))
            values = jnp.concatenate(
                [
                    jnp.concatenate([v[own, lanes] * mask, one], axis=1)
                    for mask, one in zip(masks, ones, strict=True)
                ],
                axis=0,
            )
            result = dot(jnp.concatenate(tops, axis=1), values)
            o_ref[own, lanes] = (result[:, :pair] / result[:, pair:]).astype(BF16)

    update = dot(o_ref[...], wo_ref[...]).astype(BF16).astype(F32)
    updated_ref[...] = (mid + update).astype(BF16).reshape(at_once, all_rows, width)
    for step, out_ref in enumerate(out_refs):
        kept = out_ref.shape[1]
        owner = lax.bitwise_xor(seq_ref[0], step)
        out_ref[...] = updated_ref[:, pl.ds(pl.multiple_of(owner * kept, kept), kept), :]


def assemble(seq_size, pieces, seq_ref, *refs):
    out_ref = refs[-1]
    rows, cols, width = out_ref.shape
    tokens = rows * cols

    def source(token):
        row = lax.div(token, cols)
        col = lax.rem(token, cols)
        at, base = 0, jnp.zeros_like(token)
        for piece in pieces:
            inner = piece // seq_size
            local = col - at
            owner = lax.bitwise_xor(lax.div(local, inner), seq_ref[0])
            here = (at + owner * inner + lax.rem(local, inner)) * rows + row
            base = jnp.where((local >= 0) & (local < piece), here, base)
            at += piece
        return base

    gathered = jnp.concatenate(
        [ref[...].reshape(-1, width) for ref in refs[: seq_size * len(pieces)]], axis=0
    )
    moved = dot(permutation(tokens, source), gathered)
    out_ref[...] = moved.astype(BF16).reshape(rows, cols, width)


def whole(shape):
    return pl.BlockSpec(shape, lambda *_: (0,) * len(shape))


def params():
    return pltpu.CompilerParams(vmem_limit_bytes=VMEM_BYTES)


def cost(flops, moved, special=0):
    return pl.CostEstimate(flops=int(flops), bytes_accessed=int(moved), transcendentals=int(special))


def on_device(
    states, row_query, row_key, row_value, row_out, col_query, col_key, col_value, col_out
):
    rows, block, width = states.shape
    pairs_size, res_size = lax.axis_size("pair"), lax.axis_size("res")
    seq_size = pairs_size * CORES
    all_rows, cols = rows * seq_size, block * res_size
    head_dim = width // HEADS
    pair = 2 * head_dim
    own_rows = rows // res_size
    half_pairs = HEADS // 2 // CORES
    core = lax.axis_index("core").astype(jnp.int32)
    seq = lax.axis_index("pair").astype(jnp.int32) * CORES + core
    part = lax.axis_index("res").astype(jnp.int32)
    swap = [(0, 1), (1, 0)]
    smem = pl.BlockSpec(memory_space=pltpu.SMEM)
    vmem = pl.BlockSpec(memory_space=pltpu.VMEM)
    anywhere = pl.BlockSpec(memory_space=pl.ANY)
    inner_all = block // seq_size
    chunks = [SLOT]
    while sum(chunks) < block:
        chunks.append(seq_size)

    def across(field, step):
        return lax.ppermute(field, "res", [(at, at ^ step) for at in range(res_size)])

    def around(field, step):
        return lax.ppermute(
            field, ("pair", "core"), [(at, at ^ step) for at in range(seq_size)]
        )

    blocks = [states]
    for step in range(1, res_size):
        share = lax.dynamic_slice_in_dim(states, (part ^ step) * own_rows, own_rows, axis=0)
        blocks.append(across(share, step))
    share_spec = pl.BlockSpec((own_rows, block, width), lambda g, at: (0, at[0], 0))
    fields = []
    for step, field in enumerate(blocks):
        place = (part ^ step).reshape(1)
        source = (lambda g, at: (at[0], 0, 0)) if step == 0 else (lambda g, at: (0, 0, 0))
        fields = pl.pallas_call(
            row_project,
            grid_spec=pltpu.PrefetchScalarGridSpec(
                num_scalar_prefetch=1,
                grid=(1,),
                in_specs=[pl.BlockSpec((own_rows, block, width), source)]
                + [whole((width, width))] * 3
                + [anywhere] * len(fields),
                out_specs=[share_spec] * 4,
            ),
            out_shape=[jax.ShapeDtypeStruct((own_rows, cols, width), BF16)] * 4,
            input_output_aliases={5 + at: at for at in range(len(fields))},
            compiler_params=params(),
            cost_estimate=cost(6 * own_rows * block * width * width, 6e6),
            name="row_project",
        )(place, field, row_query, row_key, row_value, *fields)
    q, k, v, x = fields

    def scores(base):
        spec = pl.BlockSpec((own_rows, cols, pair), lambda g, at: (0, 0, at[0] + g))
        return pl.pallas_call(
            functools.partial(row_scores, block, chunks),
            grid_spec=pltpu.PrefetchScalarGridSpec(
                num_scalar_prefetch=1,
                grid=(half_pairs,),
                in_specs=[spec, spec],
                out_specs=pl.BlockSpec((1, cols, 2 * cols), lambda g, at: (g, 0, 0)),
            ),
            out_shape=jax.ShapeDtypeStruct((half_pairs, cols, 2 * cols), F32),
            compiler_params=params(),
            cost_estimate=cost(4 * own_rows * cols * cols * pair * half_pairs, 2e6),
            name="row_scores",
        )(base.reshape(1), q, k)

    other = lax.ppermute(scores((1 - core) * half_pairs), "core", swap)
    mine = scores(core * half_pairs)
    shares = pairs_size * res_size
    partial = (mine + other).reshape(shares, half_pairs * cols // shares, 2 * cols)
    partial = lax.all_to_all(partial, ("pair", "res"), split_axis=0, concat_axis=0, tiled=True)
    prob = pl.pallas_call(
        functools.partial(row_softmax, head_dim ** (-0.5) / math.sqrt(all_rows)),
        out_shape=jax.ShapeDtypeStruct(partial.shape, BF16),
        compiler_params=params(),
        name="row_softmax",
    )(partial)
    prob = lax.all_to_all(prob, ("pair", "res"), split_axis=0, concat_axis=0, tiled=True)
    prob = prob.reshape(half_pairs, cols, 2 * cols)
    prob_other = lax.ppermute(prob, "core", swap)

    mids = pl.pallas_call(
        functools.partial(row_update, seq_size, res_size, chunks),
        in_specs=[smem] + [vmem] * 5,
        out_shape=[
            jax.ShapeDtypeStruct((own_rows * res_size * piece, width), BF16) for piece in chunks
        ],
        scratch_shapes=[pltpu.VMEM((own_rows, cols, width), BF16)],
        compiler_params=params(),
        cost_estimate=cost(3 * own_rows * cols * width * width, 8e6),
        name="row_update",
    )(core.reshape(1), prob, prob_other, v, x, row_out)

    home = []
    for piece, mid in zip(chunks, mids, strict=True):
        at_once = piece // seq_size
        tokens = mid.shape[0]
        moved = lax.all_to_all(
            mid, ("pair", "core", "res"), split_axis=0, concat_axis=0, tiled=True
        )
        updated = pl.pallas_call(
            functools.partial(column_update, at_once, own_rows),
            in_specs=[smem] + [vmem] * 5,
            out_shape=[jax.ShapeDtypeStruct((at_once, rows, width), BF16)] * seq_size,
            scratch_shapes=[
                pltpu.VMEM((tokens, width), BF16),
                pltpu.VMEM((at_once, all_rows, width), BF16),
            ],
            compiler_params=params(),
            cost_estimate=cost(10 * tokens * width * width, 8e6, tokens * all_rows * HEADS),
            name="column_update",
        )(seq.reshape(1), moved, col_query, col_key, col_value, col_out)
        home.append(
            [updated[0]] + [around(updated[step], step) for step in range(1, seq_size)]
        )

    row_step = 16
    out = []
    at = 0
    for slot in range(block // SLOT):
        pieces = []
        parts = []
        while sum(pieces) < SLOT:
            pieces.append(chunks[at])
            parts += home[at]
            at += 1
        out = [
            pl.pallas_call(
                functools.partial(assemble, seq_size, pieces),
                grid=(rows // row_step,),
                in_specs=[smem]
                + [
                    pl.BlockSpec((field.shape[0], row_step, width), lambda g: (0, g, 0))
                    for field in parts
                ]
                + [anywhere] * len(out),
                out_specs=pl.BlockSpec((row_step, SLOT, width), lambda g, slot=slot: (g, slot, 0)),
                out_shape=jax.ShapeDtypeStruct((rows, block, width), BF16),
                input_output_aliases={1 + len(parts): 0} if out else {},
                compiler_params=params(),
                name="assemble",
            )(seq.reshape(1), *parts, *out)
        ]
    return out[0]


def solution(mesh):
    seq_size, res_size = mesh.devices.shape
    split = Mesh(
        mesh.devices.reshape(seq_size // CORES, CORES, res_size), ("pair", "core", "res")
    )
    placed = P(("pair", "core"), "res", None)
    return jax.shard_map(
        on_device,
        mesh=split,
        in_specs=(placed,) + (P(),) * 8,
        out_specs=placed,
        check_vma=False,
    )
```

```python
import functools
import math

import jax
import jax.numpy as jnp
from jax import lax
from jax.experimental import pallas as pl
from jax.experimental.pallas import tpu as pltpu
from jax.sharding import Mesh
from jax.sharding import PartitionSpec as P

HEADS = 12
CORES = 2
SLOT = 16
VMEM_BYTES = 24 * 1024 * 1024
FULL_VMEM_BYTES = 64_000_000

BF16 = jnp.bfloat16
F32 = jnp.float32


def normalize(values):
    center = values - jnp.mean(values, axis=-1, keepdims=True)
    spread = jnp.mean(center * center, axis=-1, keepdims=True)
    return (center * lax.rsqrt(spread + 1e-05)).astype(BF16)


def dot(left, right):
    return jnp.dot(left, right, preferred_element_type=F32)


def dot_nt(left, right):
    return lax.dot_general(left, right, (((1,), (1,)), ((), ())), preferred_element_type=F32)


def head_masks(width, head_dim):
    lane = lax.broadcasted_iota(jnp.int32, (1, width), 1)
    first = (lax.rem(lane, 2 * head_dim) < head_dim).astype(F32)
    return first.astype(BF16), (1.0 - first).astype(BF16)


def permutation(size, source):
    wanted = source(lax.broadcasted_iota(jnp.int32, (size, size), 0))
    return (wanted == lax.broadcasted_iota(jnp.int32, (size, size), 1)).astype(F32).astype(BF16)


def row_shares(part_ref, states_any, *refs):
    out_refs, (held_ref, in_sems, out_sems) = refs[:-3], refs[-3:]
    rows = held_ref.shape[1]
    arrivals, departures = [], []
    for at, out_ref in enumerate(out_refs):
        owner = lax.bitwise_xor(part_ref[0], at + 1)
        arrivals.append(
            pltpu.make_async_copy(
                states_any.at[pl.ds(owner * rows, rows)], held_ref.at[at], in_sems.at[at]
            )
        )
        departures.append(pltpu.make_async_copy(held_ref.at[at], out_ref, out_sems.at[at]))
    for copy in arrivals:
        copy.start()
    for arrival, departure in zip(arrivals, departures, strict=True):
        arrival.wait()
        departure.start()
    for copy in departures:
        copy.wait()


def row_project(at_ref, x_ref, wq_ref, wk_ref, wv_ref, *refs):
    q_ref, k_ref, v_ref, kept_ref = refs[-4:]
    rows, block, width = x_ref.shape
    x = x_ref[...]
    kept_ref[...] = x
    normed = normalize(x.astype(F32).reshape(rows * block, width))
    for weight_ref, ref in ((wq_ref, q_ref), (wk_ref, k_ref), (wv_ref, v_ref)):
        ref[...] = dot(normed, weight_ref[...]).astype(BF16).reshape(rows, block, width)


def row_scores(block, chunks, base_ref, q_ref, k_ref, tied_ref):
    rows, cols, pair = q_ref.shape
    first, second = head_masks(pair, pair // 2)
    q = jnp.concatenate([q_ref[row] for row in range(rows)], axis=1)
    keys = jnp.concatenate(
        [
            jnp.concatenate([k_ref[row] * mask for row in range(rows)], axis=1)
            for mask in (first, second)
        ],
        axis=0,
    )
    score = dot_nt(q, keys).reshape(cols // block, block, 2 * cols)
    at = 0
    pieces = []
    for piece in chunks:
        pieces.append(score[:, at : at + piece].reshape(-1, 2 * cols))
        at += piece
    tied_ref[0] = jnp.concatenate(pieces, axis=0)


def row_softmax(scale, parts_ref, prob_ref):
    tied = parts_ref[0]
    for at in range(1, parts_ref.shape[0]):
        tied = tied + parts_ref[at]
    tied = tied * scale
    cols = tied.shape[1] // 2
    halves = []
    for half in (tied[:, :cols], tied[:, cols:]):
        top = jnp.exp(half - jnp.max(half, axis=-1, keepdims=True))
        halves.append(top / jnp.sum(top, axis=-1, keepdims=True))
    prob = jnp.concatenate(halves, axis=1).astype(BF16)
    for at in range(prob_ref.shape[0]):
        prob_ref[at] = prob


def row_update(seq_size, parts, chunks, core_ref, mine_ref, other_ref, v_ref, x_ref, wo_ref, mid_ref, o_ref):
    rows, cols, width = x_ref.shape
    head_dim = width // HEADS
    pair = 2 * head_dim
    half_pairs = HEADS // 2 // CORES
    masks = head_masks(pair, head_dim)

    for prob_ref, low in ((mine_ref, core_ref[0]), (other_ref, 1 - core_ref[0])):
        for at in range(half_pairs):
            lanes = pl.ds(pl.multiple_of((low * half_pairs + at) * pair, pair), pair)
            prob = prob_ref[at]
            for row in range(0, rows, 2):
                fields = [v_ref[row + step, :, lanes] for step in range(2)]
                values = jnp.concatenate(
                    [
                        jnp.concatenate([field * mask for field in fields], axis=1)
                        for mask in masks
                    ],
                    axis=0,
                )
                result = dot(prob, values).astype(BF16)
                o_ref[row, :, lanes] = result[:, :pair]
                o_ref[row + 1, :, lanes] = result[:, pair:]

    at = 0
    step_at = 0
    for piece in chunks:
        tokens = rows * parts * piece
        inner = piece // seq_size

        def source(token):
            row = lax.rem(token, rows)
            rest = lax.div(token, rows)
            step = lax.rem(rest, inner)
            rest = lax.div(rest, inner)
            part = lax.rem(rest, parts)
            owner = lax.div(rest, parts)
            return (row * parts + part) * piece + owner * inner + step

        attended = o_ref[:, at * parts : (at + piece) * parts, :].reshape(tokens, width)
        residual = x_ref[...].astype(F32).reshape(rows, parts, cols // parts, width)
        residual = residual[:, :, at : at + piece].reshape(tokens, width)
        mid = residual + dot(attended, wo_ref[...])
        moved = dot(permutation(tokens, source), mid.astype(BF16)).astype(BF16)
        mid_ref[:, step_at : step_at + inner] = moved.reshape(-1, inner, rows, width)
        at += piece
        step_at += inner


def column_update(first_at, seq_ref, mid_ref, wq_ref, wk_ref, wv_ref, wo_ref, *refs):
    out_refs, o_ref, updated_ref = refs[:-2], refs[-2], refs[-1]
    at_once, all_rows, width = updated_ref.shape
    head_dim = width // HEADS
    pair = 2 * head_dim
    scale = head_dim ** (-0.5)

    mid = mid_ref[:, first_at : first_at + at_once].astype(F32)
    mid = jnp.concatenate([mid[:, at].reshape(all_rows, width) for at in range(at_once)], axis=0)
    normed = normalize(mid)
    q = (dot(normed, wq_ref[...]).astype(BF16) * scale).astype(BF16)
    k = dot(normed, wk_ref[...]).astype(BF16)
    v = dot(normed, wv_ref[...]).astype(BF16)
    masks = head_masks(pair, head_dim)
    ones = [jnp.broadcast_to(mask, (all_rows, pair)) for mask in masks]

    for at in range(at_once):
        own = slice(at * all_rows, (at + 1) * all_rows)
        for head in range(HEADS // 2):
            lanes = slice(head * pair, (head + 1) * pair)
            keys = jnp.concatenate([k[own, lanes] * mask for mask in masks], axis=0)
            score = dot_nt(q[own, lanes], keys)
            tops = []
            for half in (score[:, :all_rows], score[:, all_rows:]):
                tops.append(jnp.exp(half - jnp.max(half, axis=-1, keepdims=True)).astype(BF16))
            values = jnp.concatenate(
                [
                    jnp.concatenate([v[own, lanes] * mask, one], axis=1)
                    for mask, one in zip(masks, ones, strict=True)
                ],
                axis=0,
            )
            result = dot(jnp.concatenate(tops, axis=1), values)
            o_ref[own, lanes] = (result[:, :pair] / result[:, pair:]).astype(BF16)

    update = dot(o_ref[...], wo_ref[...]).astype(BF16).astype(F32)
    updated_ref[...] = (mid + update).astype(BF16).reshape(at_once, all_rows, width)
    kept = out_refs[0].shape[2]
    for step, out_ref in enumerate(out_refs):
        for other in range(CORES):
            owner = lax.bitwise_xor(seq_ref[0], step * CORES + other)
            out_ref[other] = updated_ref[:, pl.ds(pl.multiple_of(owner * kept, kept), kept), :]


def in_order(refs, at, pairs_size):
    straight = refs[at * (pairs_size + 1) : at * (pairs_size + 1) + pairs_size]
    crossed = refs[at * (pairs_size + 1) + pairs_size]
    return [field for step in range(pairs_size) for field in (straight[step][0], crossed[step])]


def assemble(seq_size, pieces, seq_ref, *refs):
    out_ref = refs[-1]
    rows, cols, width = out_ref.shape
    tokens = rows * cols

    def source(token):
        row = lax.div(token, cols)
        col = lax.rem(token, cols)
        at, base = 0, jnp.zeros_like(token)
        for piece in pieces:
            inner = piece // seq_size
            local = col - at
            owner = lax.bitwise_xor(lax.div(local, inner), seq_ref[0])
            here = (at + owner * inner + lax.rem(local, inner)) * rows + row
            base = jnp.where((local >= 0) & (local < piece), here, base)
            at += piece
        return base

    gathered = jnp.concatenate(
        [
            field.reshape(-1, width)
            for at in range(len(pieces))
            for field in in_order(refs, at, seq_size // CORES)
        ],
        axis=0,
    )
    moved = dot(permutation(tokens, source), gathered)
    out_ref[...] = moved.astype(BF16).reshape(rows, cols, width)


def whole(shape):
    return pl.BlockSpec(shape, lambda *_: (0,) * len(shape))


def params(limit=VMEM_BYTES):
    return pltpu.CompilerParams(vmem_limit_bytes=limit)


def cost(flops, moved, special=0):
    return pl.CostEstimate(flops=int(flops), bytes_accessed=int(moved), transcendentals=int(special))


def on_device(
    states, row_query, row_key, row_value, row_out, col_query, col_key, col_value, col_out
):
    rows, block, width = states.shape
    pairs_size, res_size = lax.axis_size("pair"), lax.axis_size("res")
    seq_size = pairs_size * CORES
    all_rows, cols = rows * seq_size, block * res_size
    head_dim = width // HEADS
    pair = 2 * head_dim
    own_rows = rows // res_size
    half_pairs = HEADS // 2 // CORES
    core = lax.axis_index("core").astype(jnp.int32)
    seq = lax.axis_index("pair").astype(jnp.int32) * CORES + core
    part = lax.axis_index("res").astype(jnp.int32)
    swap = [(0, 1), (1, 0)]
    smem = pl.BlockSpec(memory_space=pltpu.SMEM)
    vmem = pl.BlockSpec(memory_space=pltpu.VMEM)
    anywhere = pl.BlockSpec(memory_space=pl.ANY)
    chunks = [SLOT] * (block // SLOT)

    def across(field, step):
        return lax.ppermute(field, "res", [(at, at ^ step) for at in range(res_size)])

    def around(field, step):
        return lax.ppermute(field, "pair", [(at, at ^ step) for at in range(pairs_size)])

    shares = pl.pallas_call(
        row_shares,
        in_specs=[smem, anywhere],
        out_specs=[anywhere] * (res_size - 1),
        out_shape=[jax.ShapeDtypeStruct((own_rows, block, width), BF16)] * (res_size - 1),
        scratch_shapes=[
            pltpu.VMEM((res_size - 1, own_rows, block, width), BF16),
            pltpu.SemaphoreType.DMA((res_size - 1,)),
            pltpu.SemaphoreType.DMA((res_size - 1,)),
        ],
        compiler_params=params(FULL_VMEM_BYTES),
        name="row_shares",
    )(part.reshape(1), states)
    blocks = [states] + [across(share, step + 1) for step, share in enumerate(shares)]
    halves = ((1 - core) * half_pairs).reshape(1), (core * half_pairs).reshape(1)
    places = [(part ^ step).reshape(1) for step in range(res_size)]
    own, halves, core_place, place, places = lax.optimization_barrier(
        (blocks[0], halves, core.reshape(1), seq.reshape(1), places)
    )
    blocks[0] = own
    share_spec = pl.BlockSpec((own_rows, block, width), lambda g, at: (0, at[0], 0))
    fields = []
    for step, field in enumerate(blocks):
        source = (lambda g, at: (at[0], 0, 0)) if step == 0 else (lambda g, at: (0, 0, 0))
        fields = pl.pallas_call(
            row_project,
            grid_spec=pltpu.PrefetchScalarGridSpec(
                num_scalar_prefetch=1,
                grid=(1,),
                in_specs=[pl.BlockSpec((own_rows, block, width), source)]
                + [whole((width, width))] * 3
                + [anywhere] * len(fields),
                out_specs=[share_spec] * 4,
            ),
            out_shape=[jax.ShapeDtypeStruct((own_rows, cols, width), BF16)] * 4,
            input_output_aliases={5 + at: at for at in range(len(fields))},
            compiler_params=params(),
            cost_estimate=cost(6 * own_rows * block * width * width, 6e6),
            name="row_project",
        )(places[step], field, row_query, row_key, row_value, *fields)
    q, k, v, x = fields

    def scores(base):
        spec = pl.BlockSpec((own_rows, cols, pair), lambda g, at: (0, 0, at[0] + g))
        return pl.pallas_call(
            functools.partial(row_scores, block, chunks),
            grid_spec=pltpu.PrefetchScalarGridSpec(
                num_scalar_prefetch=1,
                grid=(half_pairs,),
                in_specs=[spec, spec],
                out_specs=pl.BlockSpec((1, cols, 2 * cols), lambda g, at: (g, 0, 0)),
            ),
            out_shape=jax.ShapeDtypeStruct((half_pairs, cols, 2 * cols), F32),
            compiler_params=params(),
            cost_estimate=cost(4 * own_rows * cols * cols * pair * half_pairs, 2e6),
            name="row_scores",
        )(base, q, k)

    other = lax.ppermute(scores(halves[0]), "core", swap)
    mine = scores(halves[1])
    owners = pairs_size * res_size
    partial = (mine + other).reshape(owners, half_pairs * cols // owners, 2 * cols)
    partial = lax.all_to_all(partial, ("pair", "res"), split_axis=0, concat_axis=0, tiled=True)
    prob = pl.pallas_call(
        functools.partial(row_softmax, head_dim ** (-0.5) / math.sqrt(all_rows)),
        out_shape=jax.ShapeDtypeStruct(partial.shape, BF16),
        compiler_params=params(),
        name="row_softmax",
    )(partial)
    prob = lax.all_to_all(prob, ("pair", "res"), split_axis=0, concat_axis=0, tiled=True)
    prob = prob.reshape(half_pairs, cols, 2 * cols)
    prob_other = lax.ppermute(prob, "core", swap)

    mid = pl.pallas_call(
        functools.partial(row_update, seq_size, res_size, chunks),
        in_specs=[smem] + [vmem] * 5,
        out_shape=jax.ShapeDtypeStruct(
            (seq_size * res_size, block // seq_size, own_rows, width), BF16
        ),
        scratch_shapes=[pltpu.VMEM((own_rows, cols, width), BF16)],
        compiler_params=params(),
        cost_estimate=cost(3 * own_rows * cols * width * width, 8e6),
        name="row_update",
    )(core_place, prob, prob_other, v, x, row_out)

    moved = lax.all_to_all(mid, ("pair", "core", "res"), split_axis=0, concat_axis=0, tiled=True)
    home = []
    first_at = 0
    for piece in chunks:
        at_once = piece // seq_size
        tokens = at_once * all_rows
        updated = pl.pallas_call(
            functools.partial(column_update, first_at),
            in_specs=[smem] + [vmem] * 5,
            out_shape=[jax.ShapeDtypeStruct((CORES, at_once, rows, width), BF16)] * pairs_size,
            scratch_shapes=[
                pltpu.VMEM((tokens, width), BF16),
                pltpu.VMEM((at_once, all_rows, width), BF16),
            ],
            compiler_params=params(),
            cost_estimate=cost(10 * tokens * width * width, 8e6, tokens * all_rows * HEADS),
            name="column_update",
        )(place, moved, col_query, col_key, col_value, col_out)
        first_at += at_once
        arrived = [updated[0]] + [around(updated[step], step) for step in range(1, pairs_size)]
        crossed = lax.ppermute(jnp.stack([field[1] for field in arrived]), "core", swap)
        home.append(arrived + [crossed])

    row_step = 16
    out = []
    at = 0
    for slot in range(block // SLOT):
        pieces, parts, counts = [], [], []
        while sum(pieces) < SLOT:
            pieces.append(chunks[at])
            parts += home[at]
            counts += [1] * pairs_size + [pairs_size]
            at += 1
        out = [
            pl.pallas_call(
                functools.partial(assemble, seq_size, pieces),
                grid=(rows // row_step,),
                in_specs=[smem]
                + [
                    pl.BlockSpec((count, field.shape[1], row_step, width), lambda g: (0, 0, g, 0))
                    for field, count in zip(parts, counts, strict=True)
                ]
                + [anywhere] * len(out),
                out_specs=pl.BlockSpec((row_step, SLOT, width), lambda g, slot=slot: (g, slot, 0)),
                out_shape=jax.ShapeDtypeStruct((rows, block, width), BF16),
                input_output_aliases={1 + len(parts): 0} if out else {},
                compiler_params=params(),
                name="assemble",
            )(place, *parts, *out)
        ]
    return out[0]


def solution(mesh):
    seq_size, res_size = mesh.devices.shape
    split = Mesh(
        mesh.devices.reshape(seq_size // CORES, CORES, res_size), ("pair", "core", "res")
    )
    placed = P(("pair", "core"), "res", None)
    return jax.shard_map(
        on_device,
        mesh=split,
        in_specs=(placed,) + (P(),) * 8,
        out_specs=placed,
        check_vma=False,
    )
```

```python
import functools
import math

import jax
import jax.numpy as jnp
from jax import lax
from jax.experimental import pallas as pl
from jax.experimental.pallas import tpu as pltpu
from jax.sharding import Mesh
from jax.sharding import PartitionSpec as P

HEADS = 12
CORES = 2
HALVES = 2
SLOT = 16
VMEM_BYTES = 24 * 1024 * 1024
FULL_VMEM_BYTES = 64_000_000

BF16 = jnp.bfloat16
F32 = jnp.float32


def normalize(values):
    center = values - jnp.mean(values, axis=-1, keepdims=True)
    spread = jnp.mean(center * center, axis=-1, keepdims=True)
    return (center * lax.rsqrt(spread + 1e-05)).astype(BF16)


def dot(left, right):
    return jnp.dot(left, right, preferred_element_type=F32)


def dot_nt(left, right):
    return lax.dot_general(left, right, (((1,), (1,)), ((), ())), preferred_element_type=F32)


def head_masks(width, head_dim):
    lane = lax.broadcasted_iota(jnp.int32, (1, width), 1)
    first = (lax.rem(lane, 2 * head_dim) < head_dim).astype(F32)
    return first.astype(BF16), (1.0 - first).astype(BF16)


def permutation(size, source):
    wanted = source(lax.broadcasted_iota(jnp.int32, (size, size), 0))
    return (wanted == lax.broadcasted_iota(jnp.int32, (size, size), 1)).astype(F32).astype(BF16)


def row_shares(part_ref, states_any, *refs):
    out_refs, (held_ref, in_sems, out_sems) = refs[:-3], refs[-3:]
    rows = held_ref.shape[1]
    arrivals, departures = [], []
    for at, out_ref in enumerate(out_refs):
        owner = lax.bitwise_xor(part_ref[0], at + 1)
        arrivals.append(
            pltpu.make_async_copy(
                states_any.at[pl.ds(owner * rows, rows)], held_ref.at[at], in_sems.at[at]
            )
        )
        departures.append(pltpu.make_async_copy(held_ref.at[at], out_ref, out_sems.at[at]))
    for copy in arrivals:
        copy.start()
    for arrival, departure in zip(arrivals, departures, strict=True):
        arrival.wait()
        departure.start()
    for copy in departures:
        copy.wait()


def row_project(at_ref, x_ref, wq_ref, wk_ref, wv_ref, *refs):
    q_ref, k_ref, v_ref, kept_ref = refs[-4:]
    rows, cols, width = q_ref.shape
    block = x_ref.shape[1]
    x = x_ref[...] if x_ref.shape[0] == rows else x_ref[pl.ds(at_ref[0] * rows, rows)]
    place = pl.ds(pl.multiple_of(at_ref[0] * block, block), block)
    kept_ref[:, place, :] = x
    normed = normalize(x.astype(F32).reshape(rows * block, width))
    for weight_ref, ref in ((wq_ref, q_ref), (wk_ref, k_ref), (wv_ref, v_ref)):
        ref[:, place, :] = dot(normed, weight_ref[...]).astype(BF16).reshape(rows, block, width)


def row_scores(block, chunks, base_ref, q_ref, k_ref, tied_ref):
    rows, cols, width = q_ref.shape
    pair = 2 * (width // HEADS)
    masks = head_masks(pair, pair // 2)
    for step in range(tied_ref.shape[0]):
        lanes = pl.ds(pl.multiple_of((base_ref[0] + step) * pair, pair), pair)
        q = jnp.concatenate([q_ref[row, :, lanes] for row in range(rows)], axis=1)
        keys = jnp.concatenate(
            [
                jnp.concatenate([k_ref[row, :, lanes] * mask for row in range(rows)], axis=1)
                for mask in masks
            ],
            axis=0,
        )
        score = dot_nt(q, keys).reshape(cols // block, block, 2 * cols)
        at = 0
        pieces = []
        for piece in chunks:
            pieces.append(score[:, at : at + piece].reshape(-1, 2 * cols))
            at += piece
        tied_ref[step] = jnp.concatenate(pieces, axis=0)


def row_sum(parts_ref, tied_ref):
    tied = parts_ref[0]
    for at in range(1, parts_ref.shape[0]):
        tied = tied + parts_ref[at]
    tied_ref[...] = tied


def row_softmax(scale, mine_ref, other_ref, prob_ref):
    tied = (mine_ref[...] + other_ref[...]) * scale
    cols = tied.shape[1] // 2
    halves = []
    for half in (tied[:, :cols], tied[:, cols:]):
        top = jnp.exp(half - jnp.max(half, axis=-1, keepdims=True))
        halves.append(top / jnp.sum(top, axis=-1, keepdims=True))
    prob = jnp.concatenate(halves, axis=1).astype(BF16)
    for at in range(prob_ref.shape[0]):
        prob_ref[at] = prob


def row_update(seq_size, parts, chunks, core_ref, mine_ref, other_ref, v_ref, x_ref, wo_ref, mid_ref, o_ref):
    rows, cols, width = x_ref.shape
    head_dim = width // HEADS
    pair = 2 * head_dim
    half_pairs = HEADS // 2 // CORES
    masks = head_masks(pair, head_dim)

    for prob_ref, low in ((mine_ref, core_ref[0]), (other_ref, 1 - core_ref[0])):
        for at in range(half_pairs):
            lanes = pl.ds(pl.multiple_of((low * half_pairs + at) * pair, pair), pair)
            prob = prob_ref[at]
            for row in range(0, rows, 2):
                fields = [v_ref[row + step, :, lanes] for step in range(2)]
                values = jnp.concatenate(
                    [
                        jnp.concatenate([field * mask for field in fields], axis=1)
                        for mask in masks
                    ],
                    axis=0,
                )
                result = dot(prob, values).astype(BF16)
                o_ref[row, :, lanes] = result[:, :pair]
                o_ref[row + 1, :, lanes] = result[:, pair:]

    at = 0
    step_at = 0
    for piece in chunks:
        tokens = rows * parts * piece
        inner = piece // seq_size

        def source(token):
            row = lax.rem(token, rows)
            rest = lax.div(token, rows)
            step = lax.rem(rest, inner)
            rest = lax.div(rest, inner)
            part = lax.rem(rest, parts)
            owner = lax.div(rest, parts)
            return (row * parts + part) * piece + owner * inner + step

        attended = o_ref[:, at * parts : (at + piece) * parts, :].reshape(tokens, width)
        residual = x_ref[...].astype(F32).reshape(rows, parts, cols // parts, width)
        residual = residual[:, :, at : at + piece].reshape(tokens, width)
        mid = residual + dot(attended, wo_ref[...])
        moved = dot(permutation(tokens, source), mid.astype(BF16)).astype(BF16)
        mid_ref[:, step_at : step_at + inner] = moved.reshape(-1, inner, rows, width)
        at += piece
        step_at += inner


def column_update(first_at, seq_ref, mid_ref, wq_ref, wk_ref, wv_ref, wo_ref, *refs):
    out_refs, o_ref, updated_ref = refs[:-2], refs[-2], refs[-1]
    at_once, all_rows, width = updated_ref.shape
    head_dim = width // HEADS
    pair = 2 * head_dim
    scale = head_dim ** (-0.5)

    mid = mid_ref[:, first_at : first_at + at_once].astype(F32)
    mid = jnp.concatenate([mid[:, at].reshape(all_rows, width) for at in range(at_once)], axis=0)
    normed = normalize(mid)
    q = (dot(normed, wq_ref[...]).astype(BF16) * scale).astype(BF16)
    k = dot(normed, wk_ref[...]).astype(BF16)
    v = dot(normed, wv_ref[...]).astype(BF16)
    masks = head_masks(pair, head_dim)
    ones = [jnp.broadcast_to(mask, (all_rows, pair)) for mask in masks]

    for at in range(at_once):
        own = slice(at * all_rows, (at + 1) * all_rows)
        for head in range(HEADS // 2):
            lanes = slice(head * pair, (head + 1) * pair)
            keys = jnp.concatenate([k[own, lanes] * mask for mask in masks], axis=0)
            score = dot_nt(q[own, lanes], keys)
            tops = []
            for half in (score[:, :all_rows], score[:, all_rows:]):
                tops.append(jnp.exp(half - jnp.max(half, axis=-1, keepdims=True)).astype(BF16))
            values = jnp.concatenate(
                [
                    jnp.concatenate([v[own, lanes] * mask, one], axis=1)
                    for mask, one in zip(masks, ones, strict=True)
                ],
                axis=0,
            )
            result = dot(jnp.concatenate(tops, axis=1), values)
            o_ref[own, lanes] = (result[:, :pair] / result[:, pair:]).astype(BF16)

    update = dot(o_ref[...], wo_ref[...]).astype(BF16).astype(F32)
    updated_ref[...] = (mid + update).astype(BF16).reshape(at_once, all_rows, width)
    kept = out_refs[0].shape[2]
    for step, out_ref in enumerate(out_refs):
        for other in range(CORES):
            owner = lax.bitwise_xor(seq_ref[0], step * CORES + other)
            out_ref[other] = updated_ref[:, pl.ds(pl.multiple_of(owner * kept, kept), kept), :]


def in_order(refs, at, pairs_size):
    straight = refs[at * (pairs_size + 1) : at * (pairs_size + 1) + pairs_size]
    crossed = refs[at * (pairs_size + 1) + pairs_size]
    return [field for step in range(pairs_size) for field in (straight[step][0], crossed[step])]


def assemble(seq_size, pieces, seq_ref, *refs):
    out_ref = refs[-1]
    rows, cols, width = out_ref.shape
    tokens = rows * cols

    def source(token):
        row = lax.div(token, cols)
        col = lax.rem(token, cols)
        at, base = 0, jnp.zeros_like(token)
        for piece in pieces:
            inner = piece // seq_size
            local = col - at
            owner = lax.bitwise_xor(lax.div(local, inner), seq_ref[0])
            here = (at + owner * inner + lax.rem(local, inner)) * rows + row
            base = jnp.where((local >= 0) & (local < piece), here, base)
            at += piece
        return base

    gathered = jnp.concatenate(
        [
            field.reshape(-1, width)
            for at in range(len(pieces))
            for field in in_order(refs, at, seq_size // CORES)
        ],
        axis=0,
    )
    moved = dot(permutation(tokens, source), gathered)
    out_ref[...] = moved.astype(BF16).reshape(rows, cols, width)


def whole(shape):
    return pl.BlockSpec(shape, lambda *_: (0,) * len(shape))


def params(limit=VMEM_BYTES):
    return pltpu.CompilerParams(vmem_limit_bytes=limit)


def cost(flops, moved, special=0):
    return pl.CostEstimate(flops=int(flops), bytes_accessed=int(moved), transcendentals=int(special))


def on_device(
    states, row_query, row_key, row_value, row_out, col_query, col_key, col_value, col_out
):
    rows, block, width = states.shape
    pairs_size, res_size = lax.axis_size("pair"), HALVES * lax.axis_size("inner")
    seq_size = pairs_size * CORES
    all_rows, cols = rows * seq_size, block * res_size
    head_dim = width // HEADS
    pair = 2 * head_dim
    own_rows = rows // res_size
    half_pairs = HEADS // 2 // CORES
    core = lax.axis_index("core").astype(jnp.int32)
    seq = lax.axis_index("pair").astype(jnp.int32) * CORES + core
    part = lax.axis_index(("half", "inner")).astype(jnp.int32)
    swap = [(0, 1), (1, 0)]
    smem = pl.BlockSpec(memory_space=pltpu.SMEM)
    vmem = pl.BlockSpec(memory_space=pltpu.VMEM)
    anywhere = pl.BlockSpec(memory_space=pl.ANY)
    chunks = [SLOT] * (block // SLOT)

    def across(field, step):
        return lax.ppermute(field, ("half", "inner"), [(at, at ^ step) for at in range(res_size)])

    def around(field, step):
        return lax.ppermute(field, "pair", [(at, at ^ step) for at in range(pairs_size)])

    shares = pl.pallas_call(
        row_shares,
        in_specs=[smem, anywhere],
        out_specs=[anywhere] * (res_size - 1),
        out_shape=[jax.ShapeDtypeStruct((own_rows, block, width), BF16)] * (res_size - 1),
        scratch_shapes=[
            pltpu.VMEM((res_size - 1, own_rows, block, width), BF16),
            pltpu.SemaphoreType.DMA((res_size - 1,)),
            pltpu.SemaphoreType.DMA((res_size - 1,)),
        ],
        compiler_params=params(FULL_VMEM_BYTES),
        name="row_shares",
    )(part.reshape(1), states)
    blocks = [states] + [across(share, step + 1) for step, share in enumerate(shares)]
    halves = ((1 - core) * half_pairs).reshape(1), (core * half_pairs).reshape(1)
    places = [(part ^ step).reshape(1) for step in range(res_size)]
    own, halves, core_place, place, places = lax.optimization_barrier(
        (blocks[0], halves, core.reshape(1), seq.reshape(1), places)
    )
    blocks[0] = own
    fields = []
    for step, field in enumerate(blocks):
        fields = pl.pallas_call(
            row_project,
            in_specs=[smem] + [vmem] * (4 + len(fields)),
            out_specs=[vmem] * 4,
            out_shape=[jax.ShapeDtypeStruct((own_rows, cols, width), BF16)] * 4,
            input_output_aliases={5 + at: at for at in range(len(fields))},
            compiler_params=params(),
            cost_estimate=cost(6 * own_rows * block * width * width, 6e6),
            name="row_project",
        )(places[step], field, row_query, row_key, row_value, *fields)
    q, k, v, x = fields

    def scores(base):
        return pl.pallas_call(
            functools.partial(row_scores, block, chunks),
            in_specs=[smem, vmem, vmem],
            out_specs=vmem,
            out_shape=jax.ShapeDtypeStruct((half_pairs, cols, 2 * cols), F32),
            compiler_params=params(),
            cost_estimate=cost(4 * own_rows * cols * cols * pair * half_pairs, 2e6),
            name="row_scores",
        )(base, q, k)

    other = lax.ppermute(scores(halves[0]), "core", swap)
    mine = scores(halves[1])
    owners = pairs_size * (res_size // HALVES)
    share = (owners, half_pairs * cols // owners, 2 * cols)
    partial = lax.all_to_all(
        (mine + other).reshape(share), ("pair", "inner"), split_axis=0, concat_axis=0, tiled=True
    )
    partial = pl.pallas_call(
        row_sum,
        in_specs=[vmem],
        out_specs=vmem,
        out_shape=jax.ShapeDtypeStruct(share[1:], F32),
        compiler_params=params(),
        name="row_sum",
    )(partial)
    prob = pl.pallas_call(
        functools.partial(row_softmax, head_dim ** (-0.5) / math.sqrt(all_rows)),
        in_specs=[vmem, vmem],
        out_specs=vmem,
        out_shape=jax.ShapeDtypeStruct(share, BF16),
        compiler_params=params(),
        name="row_softmax",
    )(partial, lax.ppermute(partial, "half", swap))
    prob = lax.all_to_all(prob, ("pair", "inner"), split_axis=0, concat_axis=0, tiled=True)
    prob = prob.reshape(half_pairs, cols, 2 * cols)
    prob_other = lax.ppermute(prob, "core", swap)

    mid = pl.pallas_call(
        functools.partial(row_update, seq_size, res_size, chunks),
        in_specs=[smem] + [vmem] * 5,
        out_shape=jax.ShapeDtypeStruct(
            (seq_size * res_size, block // seq_size, own_rows, width), BF16
        ),
        scratch_shapes=[pltpu.VMEM((own_rows, cols, width), BF16)],
        compiler_params=params(),
        cost_estimate=cost(3 * own_rows * cols * width * width, 8e6),
        name="row_update",
    )(core_place, prob, prob_other, v, x, row_out)

    moved = lax.all_to_all(
        mid, ("pair", "core", "half", "inner"), split_axis=0, concat_axis=0, tiled=True
    )
    home = []
    first_at = 0
    for piece in chunks:
        at_once = piece // seq_size
        tokens = at_once * all_rows
        updated = pl.pallas_call(
            functools.partial(column_update, first_at),
            in_specs=[smem] + [vmem] * 5,
            out_shape=[jax.ShapeDtypeStruct((CORES, at_once, rows, width), BF16)] * pairs_size,
            scratch_shapes=[
                pltpu.VMEM((tokens, width), BF16),
                pltpu.VMEM((at_once, all_rows, width), BF16),
            ],
            compiler_params=params(),
            cost_estimate=cost(10 * tokens * width * width, 8e6, tokens * all_rows * HEADS),
            name="column_update",
        )(place, moved, col_query, col_key, col_value, col_out)
        first_at += at_once
        arrived = [updated[0]] + [around(updated[step], step) for step in range(1, pairs_size)]
        crossed = lax.ppermute(jnp.stack([field[1] for field in arrived]), "core", swap)
        home.append(arrived + [crossed])

    row_step = 16
    out = []
    at = 0
    for slot in range(block // SLOT):
        pieces, parts, counts = [], [], []
        while sum(pieces) < SLOT:
            pieces.append(chunks[at])
            parts += home[at]
            counts += [1] * pairs_size + [pairs_size]
            at += 1
        out = [
            pl.pallas_call(
                functools.partial(assemble, seq_size, pieces),
                grid=(rows // row_step,),
                in_specs=[smem]
                + [
                    pl.BlockSpec((count, field.shape[1], row_step, width), lambda g: (0, 0, g, 0))
                    for field, count in zip(parts, counts, strict=True)
                ]
                + [anywhere] * len(out),
                out_specs=pl.BlockSpec((row_step, SLOT, width), lambda g, slot=slot: (g, slot, 0)),
                out_shape=jax.ShapeDtypeStruct((rows, block, width), BF16),
                input_output_aliases={1 + len(parts): 0} if out else {},
                compiler_params=params(),
                name="assemble",
            )(place, *parts, *out)
        ]
    return out[0]


def solution(mesh):
    seq_size, res_size = mesh.devices.shape
    split = Mesh(
        mesh.devices.reshape(seq_size // CORES, CORES, HALVES, res_size // HALVES),
        ("pair", "core", "half", "inner"),
    )
    placed = P(("pair", "core"), ("half", "inner"), None)
    return jax.shard_map(
        on_device,
        mesh=split,
        in_specs=(placed,) + (P(),) * 8,
        out_specs=placed,
        check_vma=False,
    )
```

```python
import functools
import math

import jax
import jax.numpy as jnp
from jax import lax
from jax.experimental import pallas as pl
from jax.experimental.pallas import tpu as pltpu
from jax.sharding import Mesh
from jax.sharding import PartitionSpec as P

HEADS = 12
CORES = 2
HALVES = 2
SLOT = 16
VMEM_BYTES = 24 * 1024 * 1024
FULL_VMEM_BYTES = 64_000_000

BF16 = jnp.bfloat16
F32 = jnp.float32


def normalize(values):
    center = values - jnp.mean(values, axis=-1, keepdims=True)
    spread = jnp.mean(center * center, axis=-1, keepdims=True)
    return (center * lax.rsqrt(spread + 1e-05)).astype(BF16)


def dot(left, right):
    return jnp.dot(left, right, preferred_element_type=F32)


def dot_nt(left, right):
    return lax.dot_general(left, right, (((1,), (1,)), ((), ())), preferred_element_type=F32)


def head_masks(width, head_dim):
    lane = lax.broadcasted_iota(jnp.int32, (1, width), 1)
    first = (lax.rem(lane, 2 * head_dim) < head_dim).astype(F32)
    return first.astype(BF16), (1.0 - first).astype(BF16)


def permutation(size, source):
    wanted = source(lax.broadcasted_iota(jnp.int32, (size, 1), 0))
    found = lax.broadcasted_iota(jnp.int32, (size, size), 1) == wanted
    return found.astype(F32).astype(BF16)


def parted(number, size):
    return lax.shift_right_logical(number, size.bit_length() - 1), lax.bitwise_and(number, size - 1)


def row_shares(part_ref, states_any, *refs):
    out_refs, (held_ref, in_sems, out_sems) = refs[:-3], refs[-3:]
    rows = held_ref.shape[1]
    arrivals, departures = [], []
    for at, out_ref in enumerate(out_refs):
        owner = lax.bitwise_xor(part_ref[0], at + 1)
        arrivals.append(
            pltpu.make_async_copy(
                states_any.at[pl.ds(owner * rows, rows)], held_ref.at[at], in_sems.at[at]
            )
        )
        departures.append(pltpu.make_async_copy(held_ref.at[at], out_ref, out_sems.at[at]))
    for copy in arrivals:
        copy.start()
    for arrival, departure in zip(arrivals, departures, strict=True):
        arrival.wait()
        departure.start()
    for copy in departures:
        copy.wait()


def row_project(count, kept, at_ref, x_ref, *refs):
    weight_refs, out_refs = refs[:count], refs[len(refs) - count - kept :]
    rows, _, width = out_refs[0].shape
    block = x_ref.shape[1]
    x = x_ref[...] if x_ref.shape[0] == rows else x_ref[pl.ds(at_ref[0] * rows, rows)]
    place = pl.ds(pl.multiple_of(at_ref[0] * block, block), block)
    if kept:
        out_refs[count][:, place, :] = x
    normed = normalize(x.astype(F32).reshape(rows * block, width))
    for weight_ref, ref in zip(weight_refs, out_refs[:count], strict=True):
        ref[:, place, :] = dot(normed, weight_ref[...]).astype(BF16).reshape(rows, block, width)


def row_scores(block, chunks, base_ref, q_ref, k_ref, tied_ref):
    rows, cols, width = q_ref.shape
    pair = 2 * (width // HEADS)
    masks = head_masks(pair, pair // 2)
    for step in range(tied_ref.shape[0]):
        lanes = pl.ds(pl.multiple_of((base_ref[0] + step) * pair, pair), pair)
        q = jnp.concatenate([q_ref[row, :, lanes] for row in range(rows)], axis=1)
        keys = jnp.concatenate(
            [
                jnp.concatenate([k_ref[row, :, lanes] * mask for row in range(rows)], axis=1)
                for mask in masks
            ],
            axis=0,
        )
        score = dot_nt(q, keys).reshape(cols // block, block, 2 * cols)
        at = 0
        pieces = []
        for piece in chunks:
            pieces.append(score[:, at : at + piece].reshape(-1, 2 * cols))
            at += piece
        tied_ref[step] = jnp.concatenate(pieces, axis=0)


def row_sum(parts_ref, tied_ref):
    tied = parts_ref[0]
    for at in range(1, parts_ref.shape[0]):
        tied = tied + parts_ref[at]
    tied_ref[...] = tied


def row_softmax(scale, mine_ref, other_ref, prob_ref):
    tied = (mine_ref[...] + other_ref[...]) * scale
    cols = tied.shape[1] // 2
    halves = []
    for half in (tied[:, :cols], tied[:, cols:]):
        top = jnp.exp(half - jnp.max(half, axis=-1, keepdims=True))
        halves.append(top / jnp.sum(top, axis=-1, keepdims=True))
    prob = jnp.concatenate(halves, axis=1).astype(BF16)
    for at in range(prob_ref.shape[0]):
        prob_ref[at] = prob


def row_attend(low_ref, prob_ref, v_ref, o_ref):
    rows, _, width = v_ref.shape
    pair = 2 * (width // HEADS)
    masks = head_masks(pair, pair // 2)
    for at in range(prob_ref.shape[0]):
        lanes = pl.ds(pl.multiple_of((low_ref[0] + at) * pair, pair), pair)
        prob = prob_ref[at]
        for row in range(0, rows, 2):
            fields = [v_ref[row + step, :, lanes] for step in range(2)]
            values = jnp.concatenate(
                [jnp.concatenate([field * mask for field in fields], axis=1) for mask in masks],
                axis=0,
            )
            result = dot(prob, values).astype(BF16)
            o_ref[row, :, lanes] = result[:, :pair]
            o_ref[row + 1, :, lanes] = result[:, pair:]


def row_update(seq_size, parts, chunks, low_ref, prob_ref, v_ref, x_ref, wo_ref, *refs):
    mid_ref, o_ref = refs[-2:]
    row_attend(low_ref, prob_ref, v_ref, o_ref)
    rows, cols, width = o_ref.shape
    at = 0
    step_at = 0
    for piece in chunks:
        tokens = rows * parts * piece
        inner = piece // seq_size

        def source(token):
            rest, row = parted(token, rows)
            rest, step = parted(rest, inner)
            owner, part = parted(rest, parts)
            return (row * parts + part) * piece + owner * inner + step

        attended = o_ref[:, at * parts : (at + piece) * parts, :].reshape(tokens, width)
        residual = x_ref[...].astype(F32).reshape(rows, parts, cols // parts, width)
        residual = residual[:, :, at : at + piece].reshape(tokens, width)
        mid = residual + dot(attended, wo_ref[...])
        moved = dot(permutation(tokens, source), mid.astype(BF16)).astype(BF16)
        mid_ref[:, step_at : step_at + inner] = moved.reshape(-1, inner, rows, width)
        at += piece
        step_at += inner


def column_update(first_at, seq_ref, mid_ref, wq_ref, wk_ref, wv_ref, wo_ref, *refs):
    out_refs, o_ref, updated_ref = refs[:-2], refs[-2], refs[-1]
    at_once, all_rows, width = updated_ref.shape
    head_dim = width // HEADS
    pair = 2 * head_dim
    scale = head_dim ** (-0.5)

    mid = mid_ref[:, first_at : first_at + at_once].astype(F32)
    mid = jnp.concatenate([mid[:, at].reshape(all_rows, width) for at in range(at_once)], axis=0)
    normed = normalize(mid)
    q = (dot(normed, wq_ref[...]).astype(BF16) * scale).astype(BF16)
    k = dot(normed, wk_ref[...]).astype(BF16)
    v = dot(normed, wv_ref[...]).astype(BF16)
    masks = head_masks(pair, head_dim)
    ones = [jnp.broadcast_to(mask, (all_rows, pair)) for mask in masks]

    for at in range(at_once):
        own = slice(at * all_rows, (at + 1) * all_rows)
        for head in range(HEADS // 2):
            lanes = slice(head * pair, (head + 1) * pair)
            keys = jnp.concatenate([k[own, lanes] * mask for mask in masks], axis=0)
            score = dot_nt(q[own, lanes], keys)
            tops = []
            for half in (score[:, :all_rows], score[:, all_rows:]):
                tops.append(jnp.exp(half - jnp.max(half, axis=-1, keepdims=True)).astype(BF16))
            values = jnp.concatenate(
                [
                    jnp.concatenate([v[own, lanes] * mask, one], axis=1)
                    for mask, one in zip(masks, ones, strict=True)
                ],
                axis=0,
            )
            result = dot(jnp.concatenate(tops, axis=1), values)
            o_ref[own, lanes] = (result[:, :pair] / result[:, pair:]).astype(BF16)

    update = dot(o_ref[...], wo_ref[...]).astype(BF16).astype(F32)
    updated_ref[...] = (mid + update).astype(BF16).reshape(at_once, all_rows, width)
    kept = out_refs[0].shape[2]
    for step, out_ref in enumerate(out_refs):
        for other in range(CORES):
            owner = lax.bitwise_xor(seq_ref[0], step * CORES + other)
            out_ref[other] = updated_ref[:, pl.ds(pl.multiple_of(owner * kept, kept), kept), :]


def in_order(refs, at, pairs_size):
    straight = refs[at * (pairs_size + 1) : at * (pairs_size + 1) + pairs_size]
    crossed = refs[at * (pairs_size + 1) + pairs_size]
    return [field for step in range(pairs_size) for field in (straight[step][0], crossed[step])]


def assemble(seq_size, pieces, seq_ref, *refs):
    out_ref = refs[-1]
    rows, cols, width = out_ref.shape
    tokens = rows * cols

    def source(token):
        row, col = parted(token, cols)
        at, base = 0, jnp.zeros_like(token)
        for piece in pieces:
            inner = piece // seq_size
            local = col - at
            owner, step = parted(local, inner)
            owner = lax.bitwise_xor(owner, seq_ref[0])
            here = (at + owner * inner + step) * rows + row
            base = jnp.where((local >= 0) & (local < piece), here, base)
            at += piece
        return base

    gathered = jnp.concatenate(
        [
            field.reshape(-1, width)
            for at in range(len(pieces))
            for field in in_order(refs, at, seq_size // CORES)
        ],
        axis=0,
    )
    moved = dot(permutation(tokens, source), gathered)
    out_ref[...] = moved.astype(BF16).reshape(rows, cols, width)


def whole(shape):
    return pl.BlockSpec(shape, lambda *_: (0,) * len(shape))


def params(limit=VMEM_BYTES):
    return pltpu.CompilerParams(vmem_limit_bytes=limit)


def cost(flops, moved, special=0):
    return pl.CostEstimate(flops=int(flops), bytes_accessed=int(moved), transcendentals=int(special))


def on_device(
    states, row_query, row_key, row_value, row_out, col_query, col_key, col_value, col_out
):
    rows, block, width = states.shape
    pairs_size, res_size = lax.axis_size("pair"), HALVES * lax.axis_size("inner")
    seq_size = pairs_size * CORES
    all_rows, cols = rows * seq_size, block * res_size
    head_dim = width // HEADS
    pair = 2 * head_dim
    own_rows = rows // res_size
    half_pairs = HEADS // 2 // CORES
    core = lax.axis_index("core").astype(jnp.int32)
    seq = lax.axis_index("pair").astype(jnp.int32) * CORES + core
    part = lax.axis_index(("half", "inner")).astype(jnp.int32)
    swap = [(0, 1), (1, 0)]
    smem = pl.BlockSpec(memory_space=pltpu.SMEM)
    vmem = pl.BlockSpec(memory_space=pltpu.VMEM)
    anywhere = pl.BlockSpec(memory_space=pl.ANY)
    chunks = [SLOT] * (block // SLOT)

    def across(field, step):
        return lax.ppermute(field, ("half", "inner"), [(at, at ^ step) for at in range(res_size)])

    def around(field, step):
        return lax.ppermute(field, "pair", [(at, at ^ step) for at in range(pairs_size)])

    shares = pl.pallas_call(
        row_shares,
        in_specs=[smem, anywhere],
        out_specs=[anywhere] * (res_size - 1),
        out_shape=[jax.ShapeDtypeStruct((own_rows, block, width), BF16)] * (res_size - 1),
        scratch_shapes=[
            pltpu.VMEM((res_size - 1, own_rows, block, width), BF16),
            pltpu.SemaphoreType.DMA((res_size - 1,)),
            pltpu.SemaphoreType.DMA((res_size - 1,)),
        ],
        compiler_params=params(FULL_VMEM_BYTES),
        name="row_shares",
    )(part.reshape(1), states)
    blocks = [states] + [across(share, step + 1) for step, share in enumerate(shares)]
    halves = ((1 - core) * half_pairs).reshape(1), (core * half_pairs).reshape(1)
    places = [(part ^ step).reshape(1) for step in range(res_size)]
    own, halves, place, places = lax.optimization_barrier(
        (blocks[0], halves, seq.reshape(1), places)
    )
    blocks[0] = own
    def projected(step, weights, fields, kept):
        count = len(weights) + kept
        return pl.pallas_call(
            functools.partial(row_project, len(weights), kept),
            in_specs=[smem] + [vmem] * (1 + len(weights) + len(fields)),
            out_specs=[vmem] * count,
            out_shape=[jax.ShapeDtypeStruct((own_rows, cols, width), BF16)] * count,
            input_output_aliases={2 + len(weights) + at: at for at in range(len(fields))},
            compiler_params=params(),
            cost_estimate=cost(2 * len(weights) * own_rows * block * width * width, 6e6),
            name="row_project",
        )(places[step], blocks[step], *weights, *fields)

    last = res_size - 1
    fields = []
    for step in range(last):
        fields = projected(step, [row_query, row_key, row_value], fields, 1)
    q, k = projected(last, [row_query, row_key], fields[:2], 0)

    def scores(base):
        return pl.pallas_call(
            functools.partial(row_scores, block, chunks),
            in_specs=[smem, vmem, vmem],
            out_specs=vmem,
            out_shape=jax.ShapeDtypeStruct((half_pairs, cols, 2 * cols), F32),
            compiler_params=params(),
            cost_estimate=cost(4 * own_rows * cols * cols * pair * half_pairs, 2e6),
            name="row_scores",
        )(base, q, k)

    other = lax.ppermute(scores(halves[0]), "core", swap)
    mine = scores(halves[1])
    owners = pairs_size * (res_size // HALVES)
    share = (owners, half_pairs * cols // owners, 2 * cols)
    partial = lax.all_to_all(
        (mine + other).reshape(share), ("pair", "inner"), split_axis=0, concat_axis=0, tiled=True
    )
    partial = pl.pallas_call(
        row_sum,
        in_specs=[vmem],
        out_specs=vmem,
        out_shape=jax.ShapeDtypeStruct(share[1:], F32),
        compiler_params=params(),
        name="row_sum",
    )(partial)
    partial, fields = lax.optimization_barrier((partial, fields[2:]))
    v, x = projected(last, [row_value], fields, 1)
    prob = pl.pallas_call(
        functools.partial(row_softmax, head_dim ** (-0.5) / math.sqrt(all_rows)),
        in_specs=[vmem, vmem],
        out_specs=vmem,
        out_shape=jax.ShapeDtypeStruct(share, BF16),
        compiler_params=params(),
        name="row_softmax",
    )(partial, lax.ppermute(partial, "half", swap))
    prob, v = lax.optimization_barrier((prob, v))
    prob = lax.all_to_all(prob, ("pair", "inner"), split_axis=0, concat_axis=0, tiled=True)
    prob = prob.reshape(half_pairs, cols, 2 * cols)
    prob_other = lax.ppermute(prob, "core", swap)

    attended = pl.pallas_call(
        row_attend,
        in_specs=[smem, vmem, vmem],
        out_specs=vmem,
        out_shape=jax.ShapeDtypeStruct((own_rows, cols, width), BF16),
        compiler_params=params(),
        cost_estimate=cost(2 * own_rows * cols * cols * width, 3e6),
        name="row_attend",
    )(halves[1], prob, v)
    mid, _ = pl.pallas_call(
        functools.partial(row_update, seq_size, res_size, chunks),
        in_specs=[smem] + [vmem] * 5,
        out_specs=[vmem, vmem],
        out_shape=[
            jax.ShapeDtypeStruct(
                (seq_size * res_size, block // seq_size, own_rows, width), BF16
            ),
            jax.ShapeDtypeStruct((own_rows, cols, width), BF16),
        ],
        input_output_aliases={5: 1},
        compiler_params=params(),
        cost_estimate=cost(2 * own_rows * cols * width * (width + cols), 8e6),
        name="row_update",
    )(halves[0], prob_other, v, x, row_out, attended)

    moved = lax.all_to_all(
        mid, ("pair", "core", "half", "inner"), split_axis=0, concat_axis=0, tiled=True
    )
    home = []
    first_at = 0
    for piece in chunks:
        at_once = piece // seq_size
        tokens = at_once * all_rows
        updated = pl.pallas_call(
            functools.partial(column_update, first_at),
            in_specs=[smem] + [vmem] * 5,
            out_shape=[jax.ShapeDtypeStruct((CORES, at_once, rows, width), BF16)] * pairs_size,
            scratch_shapes=[
                pltpu.VMEM((tokens, width), BF16),
                pltpu.VMEM((at_once, all_rows, width), BF16),
            ],
            compiler_params=params(),
            cost_estimate=cost(10 * tokens * width * width, 8e6, tokens * all_rows * HEADS),
            name="column_update",
        )(place, moved, col_query, col_key, col_value, col_out)
        first_at += at_once
        arrived = [updated[0]] + [around(updated[step], step) for step in range(1, pairs_size)]
        crossed = lax.ppermute(jnp.stack([field[1] for field in arrived]), "core", swap)
        home.append(arrived + [crossed])

    row_step = 16
    out = []
    at = 0
    for slot in range(block // SLOT):
        pieces, parts, counts = [], [], []
        while sum(pieces) < SLOT:
            pieces.append(chunks[at])
            parts += home[at]
            counts += [1] * pairs_size + [pairs_size]
            at += 1
        out = [
            pl.pallas_call(
                functools.partial(assemble, seq_size, pieces),
                grid=(rows // row_step,),
                in_specs=[smem]
                + [
                    pl.BlockSpec((count, field.shape[1], row_step, width), lambda g: (0, 0, g, 0))
                    for field, count in zip(parts, counts, strict=True)
                ]
                + [anywhere] * len(out),
                out_specs=pl.BlockSpec((row_step, SLOT, width), lambda g, slot=slot: (g, slot, 0)),
                out_shape=jax.ShapeDtypeStruct((rows, block, width), BF16),
                input_output_aliases={1 + len(parts): 0} if out else {},
                compiler_params=params(),
                name="assemble",
            )(place, *parts, *out)
        ]
    return out[0]


def solution(mesh):
    seq_size, res_size = mesh.devices.shape
    split = Mesh(
        mesh.devices.reshape(seq_size // CORES, CORES, HALVES, res_size // HALVES),
        ("pair", "core", "half", "inner"),
    )
    placed = P(("pair", "core"), ("half", "inner"), None)
    return jax.shard_map(
        on_device,
        mesh=split,
        in_specs=(placed,) + (P(),) * 8,
        out_specs=placed,
        check_vma=False,
    )
```

```python
import functools
import math

import jax
import jax.numpy as jnp
from jax import lax
from jax.experimental import pallas as pl
from jax.experimental.pallas import tpu as pltpu
from jax.sharding import Mesh
from jax.sharding import PartitionSpec as P

HEADS = 12
CORES = 2
HALVES = 2
SLOT = 16
VMEM_BYTES = 24 * 1024 * 1024
FULL_VMEM_BYTES = 64_000_000

BF16 = jnp.bfloat16
F32 = jnp.float32


def normalize(values):
    center = values - jnp.mean(values, axis=-1, keepdims=True)
    spread = jnp.mean(center * center, axis=-1, keepdims=True)
    return (center * lax.rsqrt(spread + 1e-05)).astype(BF16)


def dot(left, right):
    return jnp.dot(left, right, preferred_element_type=F32)


def dot_nt(left, right):
    return lax.dot_general(left, right, (((1,), (1,)), ((), ())), preferred_element_type=F32)


def head_masks(width, head_dim):
    lane = lax.broadcasted_iota(jnp.int32, (1, width), 1)
    first = (lax.rem(lane, 2 * head_dim) < head_dim).astype(F32)
    return first.astype(BF16), (1.0 - first).astype(BF16)


def permutation(size, source):
    wanted = source(lax.broadcasted_iota(jnp.int32, (size, 1), 0))
    found = lax.broadcasted_iota(jnp.int32, (size, size), 1) == wanted
    return found.astype(F32).astype(BF16)


def parted(number, size):
    return lax.shift_right_logical(number, size.bit_length() - 1), lax.bitwise_and(number, size - 1)


def row_shares(part_ref, states_any, *refs):
    out_refs, (held_ref, in_sems, out_sems) = refs[:-3], refs[-3:]
    rows = held_ref.shape[1]
    arrivals, departures = [], []
    for at, out_ref in enumerate(out_refs):
        owner = lax.bitwise_xor(part_ref[0], at + 1)
        arrivals.append(
            pltpu.make_async_copy(
                states_any.at[pl.ds(owner * rows, rows)], held_ref.at[at], in_sems.at[at]
            )
        )
        departures.append(pltpu.make_async_copy(held_ref.at[at], out_ref, out_sems.at[at]))
    for copy in arrivals:
        copy.start()
    for arrival, departure in zip(arrivals, departures, strict=True):
        arrival.wait()
        departure.start()
    for copy in departures:
        copy.wait()


def row_project(count, kept, at_ref, x_ref, *refs):
    weight_refs, out_refs = refs[:count], refs[len(refs) - count - kept :]
    rows, _, width = out_refs[0].shape
    block = x_ref.shape[1]
    x = x_ref[...] if x_ref.shape[0] == rows else x_ref[pl.ds(at_ref[0] * rows, rows)]
    place = pl.ds(pl.multiple_of(at_ref[0] * block, block), block)
    if kept:
        out_refs[count][:, place, :] = x
    normed = normalize(x.astype(F32).reshape(rows * block, width))
    for weight_ref, ref in zip(weight_refs, out_refs[:count], strict=True):
        ref[:, place, :] = dot(normed, weight_ref[...]).astype(BF16).reshape(rows, block, width)


def row_scores(block, chunks, base_ref, q_ref, k_ref, tied_ref):
    rows, cols, width = q_ref.shape
    pair = 2 * (width // HEADS)
    masks = head_masks(pair, pair // 2)
    for step in range(tied_ref.shape[0]):
        lanes = pl.ds(pl.multiple_of((base_ref[0] + step) * pair, pair), pair)
        q = jnp.concatenate([q_ref[row, :, lanes] for row in range(rows)], axis=1)
        keys = jnp.concatenate(
            [
                jnp.concatenate([k_ref[row, :, lanes] * mask for row in range(rows)], axis=1)
                for mask in masks
            ],
            axis=0,
        )
        score = dot_nt(q, keys).reshape(cols // block, block, 2 * cols)
        at = 0
        pieces = []
        for piece in chunks:
            pieces.append(score[:, at : at + piece].reshape(-1, 2 * cols))
            at += piece
        tied_ref[step] = jnp.concatenate(pieces, axis=0)


def row_sum(parts_ref, tied_ref):
    tied = parts_ref[0]
    for at in range(1, parts_ref.shape[0]):
        tied = tied + parts_ref[at]
    tied_ref[...] = tied


def row_softmax(scale, mine_ref, other_ref, prob_ref):
    tied = (mine_ref[...] + other_ref[...]) * scale
    cols = tied.shape[1] // 2
    halves = []
    for half in (tied[:, :cols], tied[:, cols:]):
        top = jnp.exp(half - jnp.max(half, axis=-1, keepdims=True))
        halves.append(top / jnp.sum(top, axis=-1, keepdims=True))
    prob = jnp.concatenate(halves, axis=1).astype(BF16)
    for at in range(prob_ref.shape[0]):
        prob_ref[at] = prob


def row_attend(low_ref, prob_ref, v_ref, o_ref):
    rows, _, width = v_ref.shape
    pair = 2 * (width // HEADS)
    masks = head_masks(pair, pair // 2)
    for at in range(prob_ref.shape[0]):
        lanes = pl.ds(pl.multiple_of((low_ref[0] + at) * pair, pair), pair)
        prob = prob_ref[at]
        for row in range(0, rows, 2):
            fields = [v_ref[row + step, :, lanes] for step in range(2)]
            values = jnp.concatenate(
                [jnp.concatenate([field * mask for field in fields], axis=1) for mask in masks],
                axis=0,
            )
            result = dot(prob, values).astype(BF16)
            o_ref[row, :, lanes] = result[:, :pair]
            o_ref[row + 1, :, lanes] = result[:, pair:]


def row_update(seq_size, parts, chunks, low_ref, prob_ref, v_ref, x_ref, wo_ref, *refs):
    mid_ref, o_ref = refs[-2:]
    row_attend(low_ref, prob_ref, v_ref, o_ref)
    rows, cols, width = o_ref.shape
    at = 0
    step_at = 0
    for piece in chunks:
        tokens = rows * parts * piece
        inner = piece // seq_size

        def source(token):
            rest, row = parted(token, rows)
            rest, step = parted(rest, inner)
            owner, part = parted(rest, parts)
            return (row * parts + part) * piece + owner * inner + step

        attended = o_ref[:, at * parts : (at + piece) * parts, :].reshape(tokens, width)
        residual = x_ref[...].astype(F32).reshape(rows, parts, cols // parts, width)
        residual = residual[:, :, at : at + piece].reshape(tokens, width)
        mid = residual + dot(attended, wo_ref[...])
        moved = dot(permutation(tokens, source), mid.astype(BF16)).astype(BF16)
        mid_ref[:, step_at : step_at + inner] = moved.reshape(-1, inner, rows, width)
        at += piece
        step_at += inner


def column_update(first_at, seq_ref, mid_ref, wq_ref, wk_ref, wv_ref, wo_ref, *refs):
    out_refs, o_ref, updated_ref = refs[:-2], refs[-2], refs[-1]
    at_once, all_rows, width = updated_ref.shape
    head_dim = width // HEADS
    pair = 2 * head_dim
    scale = head_dim ** (-0.5)

    mid = mid_ref[:, first_at : first_at + at_once].astype(F32)
    mid = jnp.concatenate([mid[:, at].reshape(all_rows, width) for at in range(at_once)], axis=0)
    normed = normalize(mid)
    q = (dot(normed, wq_ref[...]).astype(BF16) * scale).astype(BF16)
    k = dot(normed, wk_ref[...]).astype(BF16)
    v = dot(normed, wv_ref[...]).astype(BF16)
    masks = head_masks(pair, head_dim)
    ones = [jnp.broadcast_to(mask, (all_rows, pair)) for mask in masks]

    for at in range(at_once):
        own = slice(at * all_rows, (at + 1) * all_rows)
        for head in range(HEADS // 2):
            lanes = slice(head * pair, (head + 1) * pair)
            keys = jnp.concatenate([k[own, lanes] * mask for mask in masks], axis=0)
            score = dot_nt(q[own, lanes], keys)
            tops = []
            for half in (score[:, :all_rows], score[:, all_rows:]):
                tops.append(jnp.exp(half - jnp.max(half, axis=-1, keepdims=True)).astype(BF16))
            values = jnp.concatenate(
                [
                    jnp.concatenate([v[own, lanes] * mask, one], axis=1)
                    for mask, one in zip(masks, ones, strict=True)
                ],
                axis=0,
            )
            result = dot(jnp.concatenate(tops, axis=1), values)
            o_ref[own, lanes] = (result[:, :pair] / result[:, pair:]).astype(BF16)

    update = dot(o_ref[...], wo_ref[...]).astype(BF16).astype(F32)
    updated_ref[...] = (mid + update).astype(BF16).reshape(at_once, all_rows, width)
    kept = out_refs[0].shape[2]
    for step, out_ref in enumerate(out_refs):
        for other in range(CORES):
            owner = lax.bitwise_xor(seq_ref[0], step * CORES + other)
            out_ref[other] = updated_ref[:, pl.ds(pl.multiple_of(owner * kept, kept), kept), :]


def in_order(refs, at, pairs_size):
    straight = refs[at * (pairs_size + 1) : at * (pairs_size + 1) + pairs_size]
    crossed = refs[at * (pairs_size + 1) + pairs_size]
    return [field for step in range(pairs_size) for field in (straight[step].at[0], crossed.at[step])]


def assemble(seq_size, pieces, slot, seq_ref, *refs):
    out_any, held_ref, sems = refs[-3:]
    count = sems.shape[0]
    rows, cols, width = held_ref.shape
    rows = rows // count
    tokens = rows * cols

    def source(token):
        row, col = parted(token, cols)
        at, base = 0, jnp.zeros_like(token)
        for piece in pieces:
            inner = piece // seq_size
            local = col - at
            owner, step = parted(local, inner)
            owner = lax.bitwise_xor(owner, seq_ref[0])
            here = (at + owner * inner + step) * rows + row
            base = jnp.where((local >= 0) & (local < piece), here, base)
            at += piece
        return base

    order = permutation(tokens, source)
    copies = []
    for step in range(count):
        own = pl.ds(step * rows, rows)
        gathered = jnp.concatenate(
            [
                field[:, own].reshape(-1, width)
                for at in range(len(pieces))
                for field in in_order(refs, at, seq_size // CORES)
            ],
            axis=0,
        )
        held_ref[own] = dot(order, gathered).astype(BF16).reshape(rows, cols, width)
        copies.append(
            pltpu.make_async_copy(
                held_ref.at[own], out_any.at[own, pl.ds(slot * cols, cols)], sems.at[step]
            )
        )
        copies[-1].start()
    for copy in copies:
        copy.wait()


def params(limit=VMEM_BYTES):
    return pltpu.CompilerParams(vmem_limit_bytes=limit)


def cost(flops, moved, special=0):
    return pl.CostEstimate(flops=int(flops), bytes_accessed=int(moved), transcendentals=int(special))


def on_device(
    states, row_query, row_key, row_value, row_out, col_query, col_key, col_value, col_out
):
    rows, block, width = states.shape
    pairs_size, res_size = lax.axis_size("pair"), HALVES * lax.axis_size("inner")
    seq_size = pairs_size * CORES
    all_rows, cols = rows * seq_size, block * res_size
    head_dim = width // HEADS
    pair = 2 * head_dim
    own_rows = rows // res_size
    half_pairs = HEADS // 2 // CORES
    core = lax.axis_index("core").astype(jnp.int32)
    seq = lax.axis_index("pair").astype(jnp.int32) * CORES + core
    part = lax.axis_index(("half", "inner")).astype(jnp.int32)
    swap = [(0, 1), (1, 0)]
    smem = pl.BlockSpec(memory_space=pltpu.SMEM)
    vmem = pl.BlockSpec(memory_space=pltpu.VMEM)
    anywhere = pl.BlockSpec(memory_space=pl.ANY)
    chunks = [SLOT] * (block // SLOT)

    def across(field, step):
        return lax.ppermute(field, ("half", "inner"), [(at, at ^ step) for at in range(res_size)])

    def around(field, step):
        return lax.ppermute(field, "pair", [(at, at ^ step) for at in range(pairs_size)])

    shares = pl.pallas_call(
        row_shares,
        in_specs=[smem, anywhere],
        out_specs=[anywhere] * (res_size - 1),
        out_shape=[jax.ShapeDtypeStruct((own_rows, block, width), BF16)] * (res_size - 1),
        scratch_shapes=[
            pltpu.VMEM((res_size - 1, own_rows, block, width), BF16),
            pltpu.SemaphoreType.DMA((res_size - 1,)),
            pltpu.SemaphoreType.DMA((res_size - 1,)),
        ],
        compiler_params=params(FULL_VMEM_BYTES),
        name="row_shares",
    )(part.reshape(1), states)
    blocks = [states, None] + [across(share, step + 2) for step, share in enumerate(shares[1:])]
    halves = ((1 - core) * half_pairs).reshape(1), (core * half_pairs).reshape(1)
    places = [(part ^ step).reshape(1) for step in range(res_size)]
    own, halves, place, places = lax.optimization_barrier(
        (blocks[0], halves, seq.reshape(1), places)
    )
    blocks[0] = own
    def projected(step, weights, fields, kept):
        count = len(weights) + kept
        return pl.pallas_call(
            functools.partial(row_project, len(weights), kept),
            in_specs=[smem] + [vmem] * (1 + len(weights) + len(fields)),
            out_specs=[vmem] * count,
            out_shape=[jax.ShapeDtypeStruct((own_rows, cols, width), BF16)] * count,
            input_output_aliases={2 + len(weights) + at: at for at in range(len(fields))},
            compiler_params=params(),
            cost_estimate=cost(2 * len(weights) * own_rows * block * width * width, 6e6),
            name="row_project",
        )(places[step], blocks[step], *weights, *fields)

    *early, last = [0, res_size - 1] + list(range(1, res_size - 1))
    fields = []
    for step in early:
        fields = projected(step, [row_query, row_key, row_value], fields, 1)
        if step == 0:
            near, fields = lax.optimization_barrier((shares[0], fields))
            blocks[1] = across(near, 1)
    q, k = projected(last, [row_query, row_key], fields[:2], 0)

    def scores(base):
        return pl.pallas_call(
            functools.partial(row_scores, block, chunks),
            in_specs=[smem, vmem, vmem],
            out_specs=vmem,
            out_shape=jax.ShapeDtypeStruct((half_pairs, cols, 2 * cols), F32),
            compiler_params=params(),
            cost_estimate=cost(4 * own_rows * cols * cols * pair * half_pairs, 2e6),
            name="row_scores",
        )(base, q, k)

    other = lax.ppermute(scores(halves[0]), "core", swap)
    mine = scores(halves[1])
    owners = pairs_size * (res_size // HALVES)
    share = (owners, half_pairs * cols // owners, 2 * cols)
    partial = lax.all_to_all(
        (mine + other).reshape(share), ("pair", "inner"), split_axis=0, concat_axis=0, tiled=True
    )
    partial = pl.pallas_call(
        row_sum,
        in_specs=[vmem],
        out_specs=vmem,
        out_shape=jax.ShapeDtypeStruct(share[1:], F32),
        compiler_params=params(),
        name="row_sum",
    )(partial)
    partial, fields = lax.optimization_barrier((partial, fields[2:]))
    v, x = projected(last, [row_value], fields, 1)
    prob = pl.pallas_call(
        functools.partial(row_softmax, head_dim ** (-0.5) / math.sqrt(all_rows)),
        in_specs=[vmem, vmem],
        out_specs=vmem,
        out_shape=jax.ShapeDtypeStruct(share, BF16),
        compiler_params=params(),
        name="row_softmax",
    )(partial, lax.ppermute(partial, "half", swap))
    prob, v = lax.optimization_barrier((prob, v))
    prob = lax.all_to_all(prob, ("pair", "inner"), split_axis=0, concat_axis=0, tiled=True)
    prob = prob.reshape(half_pairs, cols, 2 * cols)
    prob_other = lax.ppermute(prob, "core", swap)

    attended = pl.pallas_call(
        row_attend,
        in_specs=[smem, vmem, vmem],
        out_specs=vmem,
        out_shape=jax.ShapeDtypeStruct((own_rows, cols, width), BF16),
        compiler_params=params(),
        cost_estimate=cost(2 * own_rows * cols * cols * width, 3e6),
        name="row_attend",
    )(halves[1], prob, v)
    mid, _ = pl.pallas_call(
        functools.partial(row_update, seq_size, res_size, chunks),
        in_specs=[smem] + [vmem] * 5,
        out_specs=[vmem, vmem],
        out_shape=[
            jax.ShapeDtypeStruct(
                (seq_size * res_size, block // seq_size, own_rows, width), BF16
            ),
            jax.ShapeDtypeStruct((own_rows, cols, width), BF16),
        ],
        input_output_aliases={5: 1},
        compiler_params=params(),
        cost_estimate=cost(2 * own_rows * cols * width * (width + cols), 8e6),
        name="row_update",
    )(halves[0], prob_other, v, x, row_out, attended)

    moved = lax.all_to_all(
        mid, ("pair", "core", "half", "inner"), split_axis=0, concat_axis=0, tiled=True
    )
    home = []
    first_at = 0
    for piece in chunks:
        at_once = piece // seq_size
        tokens = at_once * all_rows
        updated = pl.pallas_call(
            functools.partial(column_update, first_at),
            in_specs=[smem] + [vmem] * 5,
            out_shape=[jax.ShapeDtypeStruct((CORES, at_once, rows, width), BF16)] * pairs_size,
            scratch_shapes=[
                pltpu.VMEM((tokens, width), BF16),
                pltpu.VMEM((at_once, all_rows, width), BF16),
            ],
            compiler_params=params(),
            cost_estimate=cost(10 * tokens * width * width, 8e6, tokens * all_rows * HEADS),
            name="column_update",
        )(place, moved, col_query, col_key, col_value, col_out)
        first_at += at_once
        arrived = [updated[0]] + [around(updated[step], step) for step in range(1, pairs_size)]
        crossed = lax.ppermute(jnp.stack([field[1] for field in arrived]), "core", swap)
        home.append(arrived + [crossed])

    steps = 2
    out = []
    at = 0
    for slot in range(block // SLOT):
        pieces, parts = [], []
        while sum(pieces) < SLOT:
            pieces.append(chunks[at])
            parts += home[at]
            at += 1
        out = [
            pl.pallas_call(
                functools.partial(assemble, seq_size, pieces, slot),
                in_specs=[smem] + [vmem] * len(parts) + [anywhere] * len(out),
                out_specs=anywhere,
                out_shape=jax.ShapeDtypeStruct((rows, block, width), BF16),
                input_output_aliases={1 + len(parts): 0} if out else {},
                scratch_shapes=[
                    pltpu.VMEM((rows, SLOT, width), BF16),
                    pltpu.SemaphoreType.DMA((steps,)),
                ],
                compiler_params=params(),
                name="assemble",
            )(place, *parts, *out)
        ]
    return out[0]


def solution(mesh):
    seq_size, res_size = mesh.devices.shape
    split = Mesh(
        mesh.devices.reshape(seq_size // CORES, CORES, HALVES, res_size // HALVES),
        ("pair", "core", "half", "inner"),
    )
    placed = P(("pair", "core"), ("half", "inner"), None)
    return jax.shard_map(
        on_device,
        mesh=split,
        in_specs=(placed,) + (P(),) * 8,
        out_specs=placed,
        check_vma=False,
    )
```

```python
import functools
import math

import jax
import jax.numpy as jnp
from jax import lax
from jax.experimental import pallas as pl
from jax.experimental.pallas import tpu as pltpu
from jax.sharding import Mesh
from jax.sharding import PartitionSpec as P

HEADS = 12
CORES = 2
HALVES = 2
SLOT = 16
VMEM_BYTES = 24 * 1024 * 1024
FULL_VMEM_BYTES = 64_000_000

BF16 = jnp.bfloat16
F32 = jnp.float32


def normalize(values):
    center = values - jnp.mean(values, axis=-1, keepdims=True)
    spread = jnp.mean(center * center, axis=-1, keepdims=True)
    return (center * lax.rsqrt(spread + 1e-05)).astype(BF16)


def dot(left, right):
    return jnp.dot(left, right, preferred_element_type=F32)


def dot_nt(left, right):
    return lax.dot_general(left, right, (((1,), (1,)), ((), ())), preferred_element_type=F32)


def head_masks(width, head_dim):
    lane = lax.broadcasted_iota(jnp.int32, (1, width), 1)
    first = (lax.rem(lane, 2 * head_dim) < head_dim).astype(F32)
    return first.astype(BF16), (1.0 - first).astype(BF16)


def permutation(size, source):
    wanted = source(lax.broadcasted_iota(jnp.int32, (size, 1), 0))
    found = lax.broadcasted_iota(jnp.int32, (size, size), 1) == wanted
    return found.astype(F32).astype(BF16)


def parted(number, size):
    return lax.shift_right_logical(number, size.bit_length() - 1), lax.bitwise_and(number, size - 1)


def row_shares(part_ref, states_any, *refs):
    out_refs, (held_ref, in_sems, out_sems) = refs[:-3], refs[-3:]
    rows = held_ref.shape[1]
    arrivals, departures = [], []
    for at, out_ref in enumerate(out_refs):
        owner = lax.bitwise_xor(part_ref[0], at + 1)
        arrivals.append(
            pltpu.make_async_copy(
                states_any.at[pl.ds(owner * rows, rows)], held_ref.at[at], in_sems.at[at]
            )
        )
        departures.append(pltpu.make_async_copy(held_ref.at[at], out_ref, out_sems.at[at]))
    for copy in arrivals:
        copy.start()
    for arrival, departure in zip(arrivals, departures, strict=True):
        arrival.wait()
        departure.start()
    for copy in departures:
        copy.wait()


def row_project(count, kept, at_ref, x_ref, *refs):
    weight_refs, out_refs = refs[:count], refs[len(refs) - count - kept :]
    rows, _, width = out_refs[0].shape
    block = x_ref.shape[1]
    x = x_ref[...] if x_ref.shape[0] == rows else x_ref[pl.ds(at_ref[0] * rows, rows)]
    place = pl.ds(pl.multiple_of(at_ref[0] * block, block), block)
    if kept:
        out_refs[count][:, place, :] = x
    normed = normalize(x.astype(F32).reshape(rows * block, width))
    for weight_ref, ref in zip(weight_refs, out_refs[:count], strict=True):
        ref[:, place, :] = dot(normed, weight_ref[...]).astype(BF16).reshape(rows, block, width)


def row_scores(block, chunks, base_ref, q_ref, k_ref, tied_ref):
    rows, cols, width = q_ref.shape
    pair = 2 * (width // HEADS)
    masks = head_masks(pair, pair // 2)
    for step in range(tied_ref.shape[0]):
        lanes = pl.ds(pl.multiple_of((base_ref[0] + step) * pair, pair), pair)
        q = jnp.concatenate([q_ref[row, :, lanes] for row in range(rows)], axis=1)
        keys = jnp.concatenate(
            [
                jnp.concatenate([k_ref[row, :, lanes] * mask for row in range(rows)], axis=1)
                for mask in masks
            ],
            axis=0,
        )
        score = dot_nt(q, keys).reshape(cols // block, block, 2 * cols)
        at = 0
        pieces = []
        for piece in chunks:
            pieces.append(score[:, at : at + piece].reshape(-1, 2 * cols))
            at += piece
        tied_ref[step] = jnp.concatenate(pieces, axis=0)


def row_sum(parts_ref, tied_ref):
    tied = parts_ref[0]
    for at in range(1, parts_ref.shape[0]):
        tied = tied + parts_ref[at]
    tied_ref[...] = tied


def row_softmax(scale, mine_ref, other_ref, prob_ref):
    tied = (mine_ref[...] + other_ref[...]) * scale
    cols = tied.shape[1] // 2
    halves = []
    for half in (tied[:, :cols], tied[:, cols:]):
        top = jnp.exp(half - jnp.max(half, axis=-1, keepdims=True))
        halves.append(top / jnp.sum(top, axis=-1, keepdims=True))
    prob = jnp.concatenate(halves, axis=1).astype(BF16)
    for at in range(prob_ref.shape[0]):
        prob_ref[at] = prob


def moved_order(rows, parts, piece, inner):
    def source(token):
        rest, row = parted(token, rows)
        rest, step = parted(rest, inner)
        owner, part = parted(rest, parts)
        return (row * parts + part) * piece + owner * inner + step

    return permutation(rows * parts * piece, source)


def row_attend(seq_size, parts, low_ref, prob_ref, v_ref, o_ref, held_ref):
    rows, _, width = v_ref.shape
    pair = 2 * (width // HEADS)
    count = prob_ref.shape[0]
    masks = head_masks(pair, pair // 2)
    for at in range(count):
        lanes = pl.ds(pl.multiple_of((low_ref[0] + at) * pair, pair), pair)
        own = slice(at * pair, (at + 1) * pair)
        prob = prob_ref[at]
        for row in range(0, rows, 2):
            fields = [v_ref[row + step, :, lanes] for step in range(2)]
            values = jnp.concatenate(
                [jnp.concatenate([field * mask for field in fields], axis=1) for mask in masks],
                axis=0,
            )
            result = dot(prob, values).astype(BF16)
            held_ref[row, :, own] = result[:, :pair]
            held_ref[row + 1, :, own] = result[:, pair:]
    lanes = pl.ds(pl.multiple_of(low_ref[0] * pair, pair), count * pair)
    order = moved_order(rows, parts, SLOT, SLOT // seq_size)
    tokens = o_ref.shape[1]
    for chunk in range(o_ref.shape[0]):
        field = held_ref[:, chunk * SLOT * parts : (chunk + 1) * SLOT * parts, :]
        o_ref[chunk, :, lanes] = dot(order, field.reshape(tokens, count * pair)).astype(BF16)


def row_keep(seq_size, parts, x_ref, kept_ref):
    rows, cols, width = x_ref.shape
    order = moved_order(rows, parts, SLOT, SLOT // seq_size)
    for chunk in range(kept_ref.shape[0]):
        field = x_ref[...].reshape(rows, parts, cols // parts, width)
        field = field[:, :, chunk * SLOT : (chunk + 1) * SLOT].reshape(-1, width)
        kept_ref[chunk] = dot(order, field).astype(BF16)


def row_update(seq_size, parts, low_ref, prob_ref, v_ref, kept_ref, wo_ref, _, mid_ref, o_ref, held_ref):
    row_attend(seq_size, parts, low_ref, prob_ref, v_ref, o_ref, held_ref)
    _, _, rows, width = mid_ref.shape
    inner = SLOT // seq_size
    for chunk in range(o_ref.shape[0]):
        mid = kept_ref[chunk].astype(F32) + dot(o_ref[chunk], wo_ref[...])
        own = slice(chunk * inner, (chunk + 1) * inner)
        mid_ref[:, own] = mid.astype(BF16).reshape(-1, inner, rows, width)


def column_update(first_at, seq_ref, mid_ref, wq_ref, wk_ref, wv_ref, wo_ref, *refs):
    out_refs, o_ref, updated_ref = refs[:-2], refs[-2], refs[-1]
    at_once, all_rows, width = updated_ref.shape
    head_dim = width // HEADS
    pair = 2 * head_dim
    scale = head_dim ** (-0.5)

    mid = mid_ref[:, first_at : first_at + at_once].astype(F32)
    mid = jnp.concatenate([mid[:, at].reshape(all_rows, width) for at in range(at_once)], axis=0)
    normed = normalize(mid)
    q = (dot(normed, wq_ref[...]).astype(BF16) * scale).astype(BF16)
    k = dot(normed, wk_ref[...]).astype(BF16)
    v = dot(normed, wv_ref[...]).astype(BF16)
    masks = head_masks(pair, head_dim)
    ones = [jnp.broadcast_to(mask, (all_rows, pair)) for mask in masks]

    for at in range(at_once):
        own = slice(at * all_rows, (at + 1) * all_rows)
        for head in range(HEADS // 2):
            lanes = slice(head * pair, (head + 1) * pair)
            keys = jnp.concatenate([k[own, lanes] * mask for mask in masks], axis=0)
            score = dot_nt(q[own, lanes], keys)
            tops = []
            for half in (score[:, :all_rows], score[:, all_rows:]):
                tops.append(jnp.exp(half - jnp.max(half, axis=-1, keepdims=True)).astype(BF16))
            values = jnp.concatenate(
                [
                    jnp.concatenate([v[own, lanes] * mask, one], axis=1)
                    for mask, one in zip(masks, ones, strict=True)
                ],
                axis=0,
            )
            result = dot(jnp.concatenate(tops, axis=1), values)
            o_ref[own, lanes] = (result[:, :pair] / result[:, pair:]).astype(BF16)

    update = dot(o_ref[...], wo_ref[...]).astype(BF16).astype(F32)
    updated_ref[...] = (mid + update).astype(BF16).reshape(at_once, all_rows, width)
    kept = out_refs[0].shape[2]
    for step, out_ref in enumerate(out_refs):
        for other in range(CORES):
            owner = lax.bitwise_xor(seq_ref[0], step * CORES + other)
            out_ref[other] = updated_ref[:, pl.ds(pl.multiple_of(owner * kept, kept), kept), :]


def in_order(refs, at, pairs_size):
    straight = refs[at * (pairs_size + 1) : at * (pairs_size + 1) + pairs_size]
    crossed = refs[at * (pairs_size + 1) + pairs_size]
    return [field for step in range(pairs_size) for field in (straight[step].at[0], crossed.at[step])]


def assemble(seq_size, pieces, slot, seq_ref, *refs):
    out_any, held_ref, sems = refs[-3:]
    count = sems.shape[0]
    rows, cols, width = held_ref.shape
    rows = rows // count
    tokens = rows * cols

    def source(token):
        row, col = parted(token, cols)
        at, base = 0, jnp.zeros_like(token)
        for piece in pieces:
            inner = piece // seq_size
            local = col - at
            owner, step = parted(local, inner)
            owner = lax.bitwise_xor(owner, seq_ref[0])
            here = (at + owner * inner + step) * rows + row
            base = jnp.where((local >= 0) & (local < piece), here, base)
            at += piece
        return base

    order = permutation(tokens, source)
    copies = []
    for step in range(count):
        own = pl.ds(step * rows, rows)
        gathered = jnp.concatenate(
            [
                field[:, own].reshape(-1, width)
                for at in range(len(pieces))
                for field in in_order(refs, at, seq_size // CORES)
            ],
            axis=0,
        )
        held_ref[own] = dot(order, gathered).astype(BF16).reshape(rows, cols, width)
        copies.append(
            pltpu.make_async_copy(
                held_ref.at[own], out_any.at[own, pl.ds(slot * cols, cols)], sems.at[step]
            )
        )
        copies[-1].start()
    for copy in copies:
        copy.wait()


def params(limit=VMEM_BYTES):
    return pltpu.CompilerParams(vmem_limit_bytes=limit)


def cost(flops, moved, special=0):
    return pl.CostEstimate(flops=int(flops), bytes_accessed=int(moved), transcendentals=int(special))


def on_device(
    states, row_query, row_key, row_value, row_out, col_query, col_key, col_value, col_out
):
    rows, block, width = states.shape
    pairs_size, res_size = lax.axis_size("pair"), HALVES * lax.axis_size("inner")
    seq_size = pairs_size * CORES
    all_rows, cols = rows * seq_size, block * res_size
    head_dim = width // HEADS
    pair = 2 * head_dim
    own_rows = rows // res_size
    half_pairs = HEADS // 2 // CORES
    core = lax.axis_index("core").astype(jnp.int32)
    seq = lax.axis_index("pair").astype(jnp.int32) * CORES + core
    part = lax.axis_index(("half", "inner")).astype(jnp.int32)
    swap = [(0, 1), (1, 0)]
    smem = pl.BlockSpec(memory_space=pltpu.SMEM)
    vmem = pl.BlockSpec(memory_space=pltpu.VMEM)
    anywhere = pl.BlockSpec(memory_space=pl.ANY)
    chunks = [SLOT] * (block // SLOT)

    def across(field, step):
        return lax.ppermute(field, ("half", "inner"), [(at, at ^ step) for at in range(res_size)])

    def around(field, step):
        return lax.ppermute(field, "pair", [(at, at ^ step) for at in range(pairs_size)])

    shares = pl.pallas_call(
        row_shares,
        in_specs=[smem, anywhere],
        out_specs=[anywhere] * (res_size - 1),
        out_shape=[jax.ShapeDtypeStruct((own_rows, block, width), BF16)] * (res_size - 1),
        scratch_shapes=[
            pltpu.VMEM((res_size - 1, own_rows, block, width), BF16),
            pltpu.SemaphoreType.DMA((res_size - 1,)),
            pltpu.SemaphoreType.DMA((res_size - 1,)),
        ],
        compiler_params=params(FULL_VMEM_BYTES),
        name="row_shares",
    )(part.reshape(1), states)
    blocks = [states, None] + [across(share, step + 2) for step, share in enumerate(shares[1:])]
    halves = ((1 - core) * half_pairs).reshape(1), (core * half_pairs).reshape(1)
    places = [(part ^ step).reshape(1) for step in range(res_size)]
    own, halves, place, places = lax.optimization_barrier(
        (blocks[0], halves, seq.reshape(1), places)
    )
    blocks[0] = own
    def projected(step, weights, fields, kept):
        count = len(weights) + kept
        return pl.pallas_call(
            functools.partial(row_project, len(weights), kept),
            in_specs=[smem] + [vmem] * (1 + len(weights) + len(fields)),
            out_specs=[vmem] * count,
            out_shape=[jax.ShapeDtypeStruct((own_rows, cols, width), BF16)] * count,
            input_output_aliases={2 + len(weights) + at: at for at in range(len(fields))},
            compiler_params=params(),
            cost_estimate=cost(2 * len(weights) * own_rows * block * width * width, 6e6),
            name="row_project",
        )(places[step], blocks[step], *weights, *fields)

    *early, last = [0, res_size - 1] + list(range(1, res_size - 1))
    fields = []
    for step in early:
        fields = projected(step, [row_query, row_key, row_value], fields, 1)
        if step == 0:
            near, fields = lax.optimization_barrier((shares[0], fields))
            blocks[1] = across(near, 1)
    q, k = projected(last, [row_query, row_key], fields[:2], 0)

    def scores(base):
        return pl.pallas_call(
            functools.partial(row_scores, block, chunks),
            in_specs=[smem, vmem, vmem],
            out_specs=vmem,
            out_shape=jax.ShapeDtypeStruct((half_pairs, cols, 2 * cols), F32),
            compiler_params=params(),
            cost_estimate=cost(4 * own_rows * cols * cols * pair * half_pairs, 2e6),
            name="row_scores",
        )(base, q, k)

    other = lax.ppermute(scores(halves[0]), "core", swap)
    mine = scores(halves[1])
    owners = pairs_size * (res_size // HALVES)
    share = (owners, half_pairs * cols // owners, 2 * cols)
    partial = lax.all_to_all(
        (mine + other).reshape(share), ("pair", "inner"), split_axis=0, concat_axis=0, tiled=True
    )
    partial = pl.pallas_call(
        row_sum,
        in_specs=[vmem],
        out_specs=vmem,
        out_shape=jax.ShapeDtypeStruct(share[1:], F32),
        compiler_params=params(),
        name="row_sum",
    )(partial)
    partial, fields = lax.optimization_barrier((partial, fields[2:]))
    v, x = projected(last, [row_value], fields, 1)
    moved_shape = (len(chunks), own_rows * res_size * SLOT, width)
    kept = pl.pallas_call(
        functools.partial(row_keep, seq_size, res_size),
        in_specs=[vmem],
        out_specs=vmem,
        out_shape=jax.ShapeDtypeStruct(moved_shape, BF16),
        compiler_params=params(),
        cost_estimate=cost(2 * own_rows * cols * width * 512, 3e6),
        name="row_keep",
    )(x)
    prob = pl.pallas_call(
        functools.partial(row_softmax, head_dim ** (-0.5) / math.sqrt(all_rows)),
        in_specs=[vmem, vmem],
        out_specs=vmem,
        out_shape=jax.ShapeDtypeStruct(share, BF16),
        compiler_params=params(),
        name="row_softmax",
    )(partial, lax.ppermute(partial, "half", swap))
    prob, v, kept = lax.optimization_barrier((prob, v, kept))
    prob = lax.all_to_all(prob, ("pair", "inner"), split_axis=0, concat_axis=0, tiled=True)
    prob = prob.reshape(half_pairs, cols, 2 * cols)
    prob_other = lax.ppermute(prob, "core", swap)

    held = pltpu.VMEM((own_rows, cols, width // CORES), BF16)
    attended = pl.pallas_call(
        functools.partial(row_attend, seq_size, res_size),
        in_specs=[smem, vmem, vmem],
        out_specs=vmem,
        out_shape=jax.ShapeDtypeStruct(moved_shape, BF16),
        scratch_shapes=[held],
        compiler_params=params(),
        cost_estimate=cost(2 * own_rows * cols * cols * width, 3e6),
        name="row_attend",
    )(halves[1], prob, v)
    mid, _ = pl.pallas_call(
        functools.partial(row_update, seq_size, res_size),
        in_specs=[smem] + [vmem] * 5,
        out_specs=[vmem, vmem],
        out_shape=[
            jax.ShapeDtypeStruct(
                (seq_size * res_size, block // seq_size, own_rows, width), BF16
            ),
            jax.ShapeDtypeStruct(moved_shape, BF16),
        ],
        scratch_shapes=[held],
        input_output_aliases={5: 1},
        compiler_params=params(),
        cost_estimate=cost(2 * own_rows * cols * width * (width + cols), 8e6),
        name="row_update",
    )(halves[0], prob_other, v, kept, row_out, attended)

    moved = lax.all_to_all(
        mid, ("pair", "core", "half", "inner"), split_axis=0, concat_axis=0, tiled=True
    )
    home = []
    first_at = 0
    for piece in chunks:
        at_once = piece // seq_size
        tokens = at_once * all_rows
        updated = pl.pallas_call(
            functools.partial(column_update, first_at),
            in_specs=[smem] + [vmem] * 5,
            out_shape=[jax.ShapeDtypeStruct((CORES, at_once, rows, width), BF16)] * pairs_size,
            scratch_shapes=[
                pltpu.VMEM((tokens, width), BF16),
                pltpu.VMEM((at_once, all_rows, width), BF16),
            ],
            compiler_params=params(),
            cost_estimate=cost(10 * tokens * width * width, 8e6, tokens * all_rows * HEADS),
            name="column_update",
        )(place, moved, col_query, col_key, col_value, col_out)
        first_at += at_once
        arrived = [updated[0]] + [around(updated[step], step) for step in range(1, pairs_size)]
        crossed = lax.ppermute(jnp.stack([field[1] for field in arrived]), "core", swap)
        home.append(arrived + [crossed])

    steps = 2
    out = []
    at = 0
    for slot in range(block // SLOT):
        pieces, parts = [], []
        while sum(pieces) < SLOT:
            pieces.append(chunks[at])
            parts += home[at]
            at += 1
        out = [
            pl.pallas_call(
                functools.partial(assemble, seq_size, pieces, slot),
                in_specs=[smem] + [vmem] * len(parts) + [anywhere] * len(out),
                out_specs=anywhere,
                out_shape=jax.ShapeDtypeStruct((rows, block, width), BF16),
                input_output_aliases={1 + len(parts): 0} if out else {},
                scratch_shapes=[
                    pltpu.VMEM((rows, SLOT, width), BF16),
                    pltpu.SemaphoreType.DMA((steps,)),
                ],
                compiler_params=params(),
                name="assemble",
            )(place, *parts, *out)
        ]
    return out[0]


def solution(mesh):
    seq_size, res_size = mesh.devices.shape
    split = Mesh(
        mesh.devices.reshape(seq_size // CORES, CORES, HALVES, res_size // HALVES),
        ("pair", "core", "half", "inner"),
    )
    placed = P(("pair", "core"), ("half", "inner"), None)
    return jax.shard_map(
        on_device,
        mesh=split,
        in_specs=(placed,) + (P(),) * 8,
        out_specs=placed,
        check_vma=False,
    )
```

```python
import functools
import math

import jax
import jax.numpy as jnp
from jax import lax
from jax.experimental import pallas as pl
from jax.experimental.pallas import tpu as pltpu
from jax.sharding import Mesh
from jax.sharding import PartitionSpec as P

HEADS = 12
CORES = 2
HALVES = 2
SLOT = 16
VMEM_BYTES = 24 * 1024 * 1024
FULL_VMEM_BYTES = 64_000_000

BF16 = jnp.bfloat16
F32 = jnp.float32


def normalize(values):
    center = values - jnp.mean(values, axis=-1, keepdims=True)
    spread = jnp.mean(center * center, axis=-1, keepdims=True)
    return (center * lax.rsqrt(spread + 1e-05)).astype(BF16)


def dot(left, right):
    return jnp.dot(left, right, preferred_element_type=F32)


def dot_nt(left, right):
    return lax.dot_general(left, right, (((1,), (1,)), ((), ())), preferred_element_type=F32)


def head_masks(width, head_dim):
    lane = lax.broadcasted_iota(jnp.int32, (1, width), 1)
    first = (lax.rem(lane, 2 * head_dim) < head_dim).astype(F32)
    return first.astype(BF16), (1.0 - first).astype(BF16)


def permutation(size, source):
    wanted = source(lax.broadcasted_iota(jnp.int32, (size, 1), 0))
    found = lax.broadcasted_iota(jnp.int32, (size, size), 1) == wanted
    return found.astype(F32).astype(BF16)


def parted(number, size):
    return lax.shift_right_logical(number, size.bit_length() - 1), lax.bitwise_and(number, size - 1)


def row_shares(part_ref, states_any, *refs):
    out_refs, (held_ref, in_sems, out_sems) = refs[:-3], refs[-3:]
    rows = held_ref.shape[1]
    arrivals, departures = [], []
    for at, out_ref in enumerate(out_refs):
        owner = lax.bitwise_xor(part_ref[0], at + 1)
        arrivals.append(
            pltpu.make_async_copy(
                states_any.at[pl.ds(owner * rows, rows)], held_ref.at[at], in_sems.at[at]
            )
        )
        departures.append(pltpu.make_async_copy(held_ref.at[at], out_ref, out_sems.at[at]))
    for copy in arrivals:
        copy.start()
    for arrival, departure in zip(arrivals, departures, strict=True):
        arrival.wait()
        departure.start()
    for copy in departures:
        copy.wait()


def row_project(count, kept, at_ref, x_ref, *refs):
    weight_refs, out_refs = refs[:count], refs[len(refs) - count - kept :]
    rows, _, width = out_refs[0].shape
    block = x_ref.shape[1]
    x = x_ref[...] if x_ref.shape[0] == rows else x_ref[pl.ds(at_ref[0] * rows, rows)]
    place = pl.ds(pl.multiple_of(at_ref[0] * block, block), block)
    if kept:
        out_refs[count][:, place, :] = x
    normed = normalize(x.astype(F32).reshape(rows * block, width))
    for weight_ref, ref in zip(weight_refs, out_refs[:count], strict=True):
        ref[:, place, :] = dot(normed, weight_ref[...]).astype(BF16).reshape(rows, block, width)


def row_scores(block, chunks, base_ref, q_ref, k_ref, tied_ref):
    rows, cols, width = q_ref.shape
    pair = 2 * (width // HEADS)
    masks = head_masks(pair, pair // 2)
    for step in range(tied_ref.shape[0]):
        lanes = pl.ds(pl.multiple_of((base_ref[0] + step) * pair, pair), pair)
        q = jnp.concatenate([q_ref[row, :, lanes] for row in range(rows)], axis=1)
        keys = jnp.concatenate(
            [
                jnp.concatenate([k_ref[row, :, lanes] * mask for row in range(rows)], axis=1)
                for mask in masks
            ],
            axis=0,
        )
        score = dot_nt(q, keys).reshape(cols // block, block, 2 * cols)
        at = 0
        pieces = []
        for piece in chunks:
            pieces.append(score[:, at : at + piece].reshape(-1, 2 * cols))
            at += piece
        tied_ref[step] = jnp.concatenate(pieces, axis=0)


def row_sum(parts_ref, tied_ref):
    tied = parts_ref[0]
    for at in range(1, parts_ref.shape[0]):
        tied = tied + parts_ref[at]
    tied_ref[...] = tied


def row_softmax(scale, mine_ref, other_ref, prob_ref):
    tied = (mine_ref[...] + other_ref[...]) * scale
    cols = tied.shape[1] // 2
    halves = []
    for half in (tied[:, :cols], tied[:, cols:]):
        top = jnp.exp(half - jnp.max(half, axis=-1, keepdims=True))
        halves.append(top / jnp.sum(top, axis=-1, keepdims=True))
    prob = jnp.concatenate(halves, axis=1).astype(BF16)
    for at in range(prob_ref.shape[0]):
        prob_ref[at] = prob


def moved_order(rows, parts, piece, inner):
    def source(token):
        rest, row = parted(token, rows)
        rest, step = parted(rest, inner)
        owner, part = parted(rest, parts)
        return (row * parts + part) * piece + owner * inner + step

    return permutation(rows * parts * piece, source)


def row_attend(seq_size, parts, low_ref, prob_ref, v_ref, o_ref, held_ref):
    rows, _, width = v_ref.shape
    pair = 2 * (width // HEADS)
    count = prob_ref.shape[0]
    masks = head_masks(pair, pair // 2)
    for at in range(count):
        lanes = pl.ds(pl.multiple_of((low_ref[0] + at) * pair, pair), pair)
        own = slice(at * pair, (at + 1) * pair)
        prob = prob_ref[at]
        for row in range(0, rows, 2):
            fields = [v_ref[row + step, :, lanes] for step in range(2)]
            values = jnp.concatenate(
                [jnp.concatenate([field * mask for field in fields], axis=1) for mask in masks],
                axis=0,
            )
            result = dot(prob, values).astype(BF16)
            held_ref[row, :, own] = result[:, :pair]
            held_ref[row + 1, :, own] = result[:, pair:]
    lanes = pl.ds(pl.multiple_of(low_ref[0] * pair, pair), count * pair)
    order = moved_order(rows, parts, SLOT, SLOT // seq_size)
    tokens = o_ref.shape[1]
    for chunk in range(o_ref.shape[0]):
        field = held_ref[:, chunk * SLOT * parts : (chunk + 1) * SLOT * parts, :]
        o_ref[chunk, :, lanes] = dot(order, field.reshape(tokens, count * pair)).astype(BF16)


def row_keep(seq_size, parts, x_ref, kept_ref):
    rows, cols, width = x_ref.shape
    order = moved_order(rows, parts, SLOT, SLOT // seq_size)
    for chunk in range(kept_ref.shape[0]):
        field = x_ref[...].reshape(rows, parts, cols // parts, width)
        field = field[:, :, chunk * SLOT : (chunk + 1) * SLOT].reshape(-1, width)
        kept_ref[chunk] = dot(order, field).astype(BF16)


def row_update(seq_size, parts, low_ref, prob_ref, v_ref, kept_ref, wo_ref, _, mid_ref, o_ref, held_ref):
    row_attend(seq_size, parts, low_ref, prob_ref, v_ref, o_ref, held_ref)
    _, _, rows, width = mid_ref.shape
    inner = SLOT // seq_size
    for chunk in range(o_ref.shape[0]):
        mid = kept_ref[chunk].astype(F32) + dot(o_ref[chunk], wo_ref[...])
        own = slice(chunk * inner, (chunk + 1) * inner)
        mid_ref[:, own] = mid.astype(BF16).reshape(-1, inner, rows, width)


def column_update(first_at, seq_ref, mid_ref, wq_ref, wk_ref, wv_ref, wo_ref, *refs):
    out_refs, o_ref, updated_ref = refs[:-2], refs[-2], refs[-1]
    at_once, all_rows, width = updated_ref.shape
    head_dim = width // HEADS
    pair = 2 * head_dim
    scale = head_dim ** (-0.5)

    mid = mid_ref[:, first_at : first_at + at_once].astype(F32)
    mid = jnp.concatenate([mid[:, at].reshape(all_rows, width) for at in range(at_once)], axis=0)
    normed = normalize(mid)
    q = (dot(normed, wq_ref[...]).astype(BF16) * scale).astype(BF16)
    k = dot(normed, wk_ref[...]).astype(BF16)
    v = dot(normed, wv_ref[...]).astype(BF16)
    masks = head_masks(pair, head_dim)
    ones = [jnp.broadcast_to(mask, (all_rows, pair)) for mask in masks]

    for at in range(at_once):
        own = slice(at * all_rows, (at + 1) * all_rows)
        for head in range(HEADS // 2):
            lanes = slice(head * pair, (head + 1) * pair)
            keys = jnp.concatenate([k[own, lanes] * mask for mask in masks], axis=0)
            score = dot_nt(q[own, lanes], keys)
            tops = []
            for half in (score[:, :all_rows], score[:, all_rows:]):
                tops.append(jnp.exp(half - jnp.max(half, axis=-1, keepdims=True)).astype(BF16))
            values = jnp.concatenate(
                [
                    jnp.concatenate([v[own, lanes] * mask, one], axis=1)
                    for mask, one in zip(masks, ones, strict=True)
                ],
                axis=0,
            )
            result = dot(jnp.concatenate(tops, axis=1), values)
            o_ref[own, lanes] = (result[:, :pair] / result[:, pair:]).astype(BF16)

    update = dot(o_ref[...], wo_ref[...]).astype(BF16).astype(F32)
    updated_ref[...] = (mid + update).astype(BF16).reshape(at_once, all_rows, width)
    kept = out_refs[0].shape[2]
    for step, out_ref in enumerate(out_refs):
        for other in range(CORES):
            owner = lax.bitwise_xor(seq_ref[0], step * CORES + other)
            out_ref[other] = updated_ref[:, pl.ds(pl.multiple_of(owner * kept, kept), kept), :]


def in_order(refs, at, pairs_size):
    straight = refs[at * (pairs_size + 1) : at * (pairs_size + 1) + pairs_size]
    crossed = refs[at * (pairs_size + 1) + pairs_size]
    return [field for step in range(pairs_size) for field in (straight[step].at[0], crossed.at[step])]


def assemble(seq_size, pieces, slot, seq_ref, *refs):
    out_any, held_ref, sems = refs[-3:]
    count = sems.shape[0]
    rows, cols, width = held_ref.shape
    rows = rows // count
    tokens = rows * cols

    def source(token):
        row, col = parted(token, cols)
        at, base = 0, jnp.zeros_like(token)
        for piece in pieces:
            inner = piece // seq_size
            local = col - at
            owner, step = parted(local, inner)
            owner = lax.bitwise_xor(owner, seq_ref[0])
            here = (at + owner * inner + step) * rows + row
            base = jnp.where((local >= 0) & (local < piece), here, base)
            at += piece
        return base

    order = permutation(tokens, source)
    copies = []
    for step in range(count):
        own = pl.ds(step * rows, rows)
        gathered = jnp.concatenate(
            [
                field[:, own].reshape(-1, width)
                for at in range(len(pieces))
                for field in in_order(refs, at, seq_size // CORES)
            ],
            axis=0,
        )
        held_ref[own] = dot(order, gathered).astype(BF16).reshape(rows, cols, width)
        copies.append(
            pltpu.make_async_copy(
                held_ref.at[own], out_any.at[own, pl.ds(slot * cols, cols)], sems.at[step]
            )
        )
        copies[-1].start()
    for copy in copies:
        copy.wait()


def params(limit=VMEM_BYTES):
    return pltpu.CompilerParams(vmem_limit_bytes=limit)


def cost(flops, moved, special=0):
    return pl.CostEstimate(flops=int(flops), bytes_accessed=int(moved), transcendentals=int(special))


def on_device(
    states, row_query, row_key, row_value, row_out, col_query, col_key, col_value, col_out
):
    rows, block, width = states.shape
    pairs_size, res_size = lax.axis_size("pair"), HALVES * lax.axis_size("inner")
    seq_size = pairs_size * CORES
    all_rows, cols = rows * seq_size, block * res_size
    head_dim = width // HEADS
    pair = 2 * head_dim
    own_rows = rows // res_size
    half_pairs = HEADS // 2 // CORES
    core = lax.axis_index("core").astype(jnp.int32)
    seq = lax.axis_index("pair").astype(jnp.int32) * CORES + core
    part = lax.axis_index(("half", "inner")).astype(jnp.int32)
    swap = [(0, 1), (1, 0)]
    smem = pl.BlockSpec(memory_space=pltpu.SMEM)
    vmem = pl.BlockSpec(memory_space=pltpu.VMEM)
    anywhere = pl.BlockSpec(memory_space=pl.ANY)
    chunks = [SLOT] * (block // SLOT)

    def across(field, step):
        return lax.ppermute(field, ("half", "inner"), [(at, at ^ step) for at in range(res_size)])

    def around(field, step):
        return lax.ppermute(field, "pair", [(at, at ^ step) for at in range(pairs_size)])

    shares = pl.pallas_call(
        row_shares,
        in_specs=[smem, anywhere],
        out_specs=[anywhere] * (res_size - 1),
        out_shape=[jax.ShapeDtypeStruct((own_rows, block, width), BF16)] * (res_size - 1),
        scratch_shapes=[
            pltpu.VMEM((res_size - 1, own_rows, block, width), BF16),
            pltpu.SemaphoreType.DMA((res_size - 1,)),
            pltpu.SemaphoreType.DMA((res_size - 1,)),
        ],
        compiler_params=params(FULL_VMEM_BYTES),
        name="row_shares",
    )(part.reshape(1), states)
    blocks = {0: states, 1: across(shares[0], 1)}
    for step in range(3, res_size):
        blocks[step] = across(shares[step - 1], step)
    halves = ((1 - core) * half_pairs).reshape(1), (core * half_pairs).reshape(1)
    places = [(part ^ step).reshape(1) for step in range(res_size)]
    own, halves, place, places = lax.optimization_barrier(
        (blocks[0], halves, seq.reshape(1), places)
    )
    blocks[0] = own
    def projected(step, weights, fields, kept):
        count = len(weights) + kept
        return pl.pallas_call(
            functools.partial(row_project, len(weights), kept),
            in_specs=[smem] + [vmem] * (1 + len(weights) + len(fields)),
            out_specs=[vmem] * count,
            out_shape=[jax.ShapeDtypeStruct((own_rows, cols, width), BF16)] * count,
            input_output_aliases={2 + len(weights) + at: at for at in range(len(fields))},
            compiler_params=params(),
            cost_estimate=cost(2 * len(weights) * own_rows * block * width * width, 6e6),
            name="row_project",
        )(places[step], blocks[step], *weights, *fields)

    *early, last = [0, res_size - 1] + list(range(1, res_size - 1))
    fields = []
    for step in early:
        fields = projected(step, [row_query, row_key, row_value], fields, 1)
        if step == 0:
            far, fields = lax.optimization_barrier((shares[1], fields))
            blocks[2] = across(far, 2)
    q, k = projected(last, [row_query, row_key], fields[:2], 0)

    def scores(base):
        return pl.pallas_call(
            functools.partial(row_scores, block, chunks),
            in_specs=[smem, vmem, vmem],
            out_specs=vmem,
            out_shape=jax.ShapeDtypeStruct((half_pairs, cols, 2 * cols), F32),
            compiler_params=params(),
            cost_estimate=cost(4 * own_rows * cols * cols * pair * half_pairs, 2e6),
            name="row_scores",
        )(base, q, k)

    other = lax.ppermute(scores(halves[0]), "core", swap)
    mine = scores(halves[1])
    owners = pairs_size * (res_size // HALVES)
    share = (owners, half_pairs * cols // owners, 2 * cols)
    partial = lax.all_to_all(
        (mine + other).reshape(share), ("pair", "inner"), split_axis=0, concat_axis=0, tiled=True
    )
    partial = pl.pallas_call(
        row_sum,
        in_specs=[vmem],
        out_specs=vmem,
        out_shape=jax.ShapeDtypeStruct(share[1:], F32),
        compiler_params=params(),
        name="row_sum",
    )(partial)
    partial, fields = lax.optimization_barrier((partial, fields[2:]))
    v, x = projected(last, [row_value], fields, 1)
    moved_shape = (len(chunks), own_rows * res_size * SLOT, width)
    kept = pl.pallas_call(
        functools.partial(row_keep, seq_size, res_size),
        in_specs=[vmem],
        out_specs=vmem,
        out_shape=jax.ShapeDtypeStruct(moved_shape, BF16),
        compiler_params=params(),
        cost_estimate=cost(2 * own_rows * cols * width * 512, 3e6),
        name="row_keep",
    )(x)
    prob = pl.pallas_call(
        functools.partial(row_softmax, head_dim ** (-0.5) / math.sqrt(all_rows)),
        in_specs=[vmem, vmem],
        out_specs=vmem,
        out_shape=jax.ShapeDtypeStruct(share, BF16),
        compiler_params=params(),
        name="row_softmax",
    )(partial, lax.ppermute(partial, "half", swap))
    prob, v, kept = lax.optimization_barrier((prob, v, kept))
    prob = lax.all_to_all(prob, ("pair", "inner"), split_axis=0, concat_axis=0, tiled=True)
    prob = prob.reshape(half_pairs, cols, 2 * cols)
    prob_other = lax.ppermute(prob, "core", swap)

    held = pltpu.VMEM((own_rows, cols, width // CORES), BF16)
    attended = pl.pallas_call(
        functools.partial(row_attend, seq_size, res_size),
        in_specs=[smem, vmem, vmem],
        out_specs=vmem,
        out_shape=jax.ShapeDtypeStruct(moved_shape, BF16),
        scratch_shapes=[held],
        compiler_params=params(),
        cost_estimate=cost(2 * own_rows * cols * cols * width, 3e6),
        name="row_attend",
    )(halves[1], prob, v)
    mid, _ = pl.pallas_call(
        functools.partial(row_update, seq_size, res_size),
        in_specs=[smem] + [vmem] * 5,
        out_specs=[vmem, vmem],
        out_shape=[
            jax.ShapeDtypeStruct(
                (seq_size * res_size, block // seq_size, own_rows, width), BF16
            ),
            jax.ShapeDtypeStruct(moved_shape, BF16),
        ],
        scratch_shapes=[held],
        input_output_aliases={5: 1},
        compiler_params=params(),
        cost_estimate=cost(2 * own_rows * cols * width * (width + cols), 8e6),
        name="row_update",
    )(halves[0], prob_other, v, kept, row_out, attended)

    moved = lax.all_to_all(
        mid, ("pair", "core", "half", "inner"), split_axis=0, concat_axis=0, tiled=True
    )
    home = []
    first_at = 0
    for piece in chunks:
        at_once = piece // seq_size
        tokens = at_once * all_rows
        updated = pl.pallas_call(
            functools.partial(column_update, first_at),
            in_specs=[smem] + [vmem] * 5,
            out_shape=[jax.ShapeDtypeStruct((CORES, at_once, rows, width), BF16)] * pairs_size,
            scratch_shapes=[
                pltpu.VMEM((tokens, width), BF16),
                pltpu.VMEM((at_once, all_rows, width), BF16),
            ],
            compiler_params=params(),
            cost_estimate=cost(10 * tokens * width * width, 8e6, tokens * all_rows * HEADS),
            name="column_update",
        )(place, moved, col_query, col_key, col_value, col_out)
        first_at += at_once
        arrived = [updated[0]] + [around(updated[step], step) for step in range(1, pairs_size)]
        crossed = lax.ppermute(jnp.stack([field[1] for field in arrived]), "core", swap)
        home.append(arrived + [crossed])

    steps = 2
    out = []
    at = 0
    for slot in range(block // SLOT):
        pieces, parts = [], []
        while sum(pieces) < SLOT:
            pieces.append(chunks[at])
            parts += home[at]
            at += 1
        out = [
            pl.pallas_call(
                functools.partial(assemble, seq_size, pieces, slot),
                in_specs=[smem] + [vmem] * len(parts) + [anywhere] * len(out),
                out_specs=anywhere,
                out_shape=jax.ShapeDtypeStruct((rows, block, width), BF16),
                input_output_aliases={1 + len(parts): 0} if out else {},
                scratch_shapes=[
                    pltpu.VMEM((rows, SLOT, width), BF16),
                    pltpu.SemaphoreType.DMA((steps,)),
                ],
                compiler_params=params(),
                name="assemble",
            )(place, *parts, *out)
        ]
    return out[0]


def solution(mesh):
    seq_size, res_size = mesh.devices.shape
    split = Mesh(
        mesh.devices.reshape(seq_size // CORES, CORES, HALVES, res_size // HALVES),
        ("pair", "core", "half", "inner"),
    )
    placed = P(("pair", "core"), ("half", "inner"), None)
    return jax.shard_map(
        on_device,
        mesh=split,
        in_specs=(placed,) + (P(),) * 8,
        out_specs=placed,
        check_vma=False,
    )
```

```python
import functools
import math

import jax
import jax.numpy as jnp
from jax import lax
from jax.experimental import pallas as pl
from jax.experimental.pallas import tpu as pltpu
from jax.sharding import Mesh
from jax.sharding import PartitionSpec as P

HEADS = 12
CORES = 2
HALVES = 2
SLOT = 16
VMEM_BYTES = 24 * 1024 * 1024
FULL_VMEM_BYTES = 64_000_000

BF16 = jnp.bfloat16
F32 = jnp.float32


def normalize(values):
    center = values - jnp.mean(values, axis=-1, keepdims=True)
    spread = jnp.mean(center * center, axis=-1, keepdims=True)
    return (center * lax.rsqrt(spread + 1e-05)).astype(BF16)


def dot(left, right):
    return jnp.dot(left, right, preferred_element_type=F32)


def dot_nt(left, right):
    return lax.dot_general(left, right, (((1,), (1,)), ((), ())), preferred_element_type=F32)


def head_masks(width, head_dim):
    lane = lax.broadcasted_iota(jnp.int32, (1, width), 1)
    first = (lax.rem(lane, 2 * head_dim) < head_dim).astype(F32)
    return first.astype(BF16), (1.0 - first).astype(BF16)


def permutation(size, source):
    wanted = source(lax.broadcasted_iota(jnp.int32, (size, 1), 0))
    found = lax.broadcasted_iota(jnp.int32, (size, size), 1) == wanted
    return found.astype(F32).astype(BF16)


def parted(number, size):
    return lax.shift_right_logical(number, size.bit_length() - 1), lax.bitwise_and(number, size - 1)


def row_shares(part_ref, states_any, *refs):
    out_refs, (held_ref, in_sems, out_sems) = refs[:-3], refs[-3:]
    rows = held_ref.shape[1]
    arrivals, departures = [], []
    for at, out_ref in enumerate(out_refs):
        owner = lax.bitwise_xor(part_ref[0], at + 1)
        arrivals.append(
            pltpu.make_async_copy(
                states_any.at[pl.ds(owner * rows, rows)], held_ref.at[at], in_sems.at[at]
            )
        )
        departures.append(pltpu.make_async_copy(held_ref.at[at], out_ref, out_sems.at[at]))
    for copy in arrivals:
        copy.start()
    for arrival, departure in zip(arrivals, departures, strict=True):
        arrival.wait()
        departure.start()
    for copy in departures:
        copy.wait()


def row_project(count, kept, at_ref, x_ref, *refs):
    weight_refs, out_refs = refs[:count], refs[len(refs) - count - kept :]
    rows, _, width = out_refs[0].shape
    block = x_ref.shape[1]
    x = x_ref[...] if x_ref.shape[0] == rows else x_ref[pl.ds(at_ref[0] * rows, rows)]
    place = pl.ds(pl.multiple_of(at_ref[0] * block, block), block)
    if kept:
        out_refs[count][:, place, :] = x
    normed = normalize(x.astype(F32).reshape(rows * block, width))
    for weight_ref, ref in zip(weight_refs, out_refs[:count], strict=True):
        ref[:, place, :] = dot(normed, weight_ref[...]).astype(BF16).reshape(rows, block, width)


def row_scores(block, chunks, base_ref, q_ref, k_ref, tied_ref):
    rows, cols, width = q_ref.shape
    pair = 2 * (width // HEADS)
    masks = head_masks(pair, pair // 2)
    for step in range(tied_ref.shape[0]):
        lanes = pl.ds(pl.multiple_of((base_ref[0] + step) * pair, pair), pair)
        q = jnp.concatenate([q_ref[row, :, lanes] for row in range(rows)], axis=1)
        keys = jnp.concatenate(
            [
                jnp.concatenate([k_ref[row, :, lanes] * mask for row in range(rows)], axis=1)
                for mask in masks
            ],
            axis=0,
        )
        score = dot_nt(q, keys).reshape(cols // block, block, 2 * cols)
        at = 0
        pieces = []
        for piece in chunks:
            pieces.append(score[:, at : at + piece].reshape(-1, 2 * cols))
            at += piece
        tied_ref[step] = jnp.concatenate(pieces, axis=0)


def row_sum(parts_ref, tied_ref):
    tied = parts_ref[0]
    for at in range(1, parts_ref.shape[0]):
        tied = tied + parts_ref[at]
    tied_ref[...] = tied


def row_softmax(scale, mine_ref, other_ref, prob_ref):
    tied = (mine_ref[...] + other_ref[...]) * scale
    cols = tied.shape[1] // 2
    halves = []
    for half in (tied[:, :cols], tied[:, cols:]):
        top = jnp.exp(half - jnp.max(half, axis=-1, keepdims=True))
        halves.append(top / jnp.sum(top, axis=-1, keepdims=True))
    prob = jnp.concatenate(halves, axis=1).astype(BF16)
    for at in range(prob_ref.shape[0]):
        prob_ref[at] = prob


def moved_order(rows, parts, piece, inner):
    def source(token):
        rest, row = parted(token, rows)
        rest, step = parted(rest, inner)
        owner, part = parted(rest, parts)
        return (row * parts + part) * piece + owner * inner + step

    return permutation(rows * parts * piece, source)


def row_attend(seq_size, parts, low_ref, prob_ref, v_ref, o_ref, held_ref):
    rows, _, width = v_ref.shape
    pair = 2 * (width // HEADS)
    count = prob_ref.shape[0]
    masks = head_masks(pair, pair // 2)
    for at in range(count):
        lanes = pl.ds(pl.multiple_of((low_ref[0] + at) * pair, pair), pair)
        own = slice(at * pair, (at + 1) * pair)
        prob = prob_ref[at]
        for row in range(0, rows, 2):
            fields = [v_ref[row + step, :, lanes] for step in range(2)]
            values = jnp.concatenate(
                [jnp.concatenate([field * mask for field in fields], axis=1) for mask in masks],
                axis=0,
            )
            result = dot(prob, values).astype(BF16)
            held_ref[row, :, own] = result[:, :pair]
            held_ref[row + 1, :, own] = result[:, pair:]
    lanes = pl.ds(pl.multiple_of(low_ref[0] * pair, pair), count * pair)
    order = moved_order(rows, parts, SLOT, SLOT // seq_size)
    tokens = o_ref.shape[1]
    for chunk in range(o_ref.shape[0]):
        field = held_ref[:, chunk * SLOT * parts : (chunk + 1) * SLOT * parts, :]
        o_ref[chunk, :, lanes] = dot(order, field.reshape(tokens, count * pair)).astype(BF16)


def row_keep(seq_size, parts, x_ref, kept_ref):
    rows, cols, width = x_ref.shape
    order = moved_order(rows, parts, SLOT, SLOT // seq_size)
    for chunk in range(kept_ref.shape[0]):
        field = x_ref[...].reshape(rows, parts, cols // parts, width)
        field = field[:, :, chunk * SLOT : (chunk + 1) * SLOT].reshape(-1, width)
        kept_ref[chunk] = dot(order, field).astype(BF16)


def row_update(seq_size, parts, low_ref, prob_ref, v_ref, kept_ref, wo_ref, _, mid_ref, o_ref, held_ref):
    row_attend(seq_size, parts, low_ref, prob_ref, v_ref, o_ref, held_ref)
    _, _, rows, width = mid_ref.shape
    inner = SLOT // seq_size
    for chunk in range(o_ref.shape[0]):
        mid = kept_ref[chunk].astype(F32) + dot(o_ref[chunk], wo_ref[...])
        own = slice(chunk * inner, (chunk + 1) * inner)
        mid_ref[:, own] = mid.astype(BF16).reshape(-1, inner, rows, width)


def column_update(first_at, seq_ref, mid_ref, wq_ref, wk_ref, wv_ref, wo_ref, *refs):
    out_refs, o_ref, updated_ref = refs[:-2], refs[-2], refs[-1]
    at_once, all_rows, width = updated_ref.shape
    head_dim = width // HEADS
    pair = 2 * head_dim
    scale = head_dim ** (-0.5)

    mid = mid_ref[:, first_at : first_at + at_once].astype(F32)
    mid = jnp.concatenate([mid[:, at].reshape(all_rows, width) for at in range(at_once)], axis=0)
    normed = normalize(mid)
    q = (dot(normed, wq_ref[...]).astype(BF16) * scale).astype(BF16)
    k = dot(normed, wk_ref[...]).astype(BF16)
    v = dot(normed, wv_ref[...]).astype(BF16)
    masks = head_masks(pair, head_dim)
    ones = [jnp.broadcast_to(mask, (all_rows, pair)) for mask in masks]

    for at in range(at_once):
        own = slice(at * all_rows, (at + 1) * all_rows)
        for head in range(HEADS // 2):
            lanes = slice(head * pair, (head + 1) * pair)
            keys = jnp.concatenate([k[own, lanes] * mask for mask in masks], axis=0)
            score = dot_nt(q[own, lanes], keys)
            tops = []
            for half in (score[:, :all_rows], score[:, all_rows:]):
                tops.append(jnp.exp(half - jnp.max(half, axis=-1, keepdims=True)).astype(BF16))
            values = jnp.concatenate(
                [
                    jnp.concatenate([v[own, lanes] * mask, one], axis=1)
                    for mask, one in zip(masks, ones, strict=True)
                ],
                axis=0,
            )
            result = dot(jnp.concatenate(tops, axis=1), values)
            o_ref[own, lanes] = (result[:, :pair] / result[:, pair:]).astype(BF16)

    update = dot(o_ref[...], wo_ref[...]).astype(BF16).astype(F32)
    updated_ref[...] = (mid + update).astype(BF16).reshape(at_once, all_rows, width)
    kept = out_refs[0].shape[2]
    for step, out_ref in enumerate(out_refs):
        for other in range(CORES):
            owner = lax.bitwise_xor(seq_ref[0], step * CORES + other)
            out_ref[other] = updated_ref[:, pl.ds(pl.multiple_of(owner * kept, kept), kept), :]


def in_order(refs, at, pairs_size):
    first = at * (pairs_size + 2)
    straight = refs[first : first + pairs_size]
    crossed = refs[first + pairs_size : first + pairs_size + 2]
    half = pairs_size // 2
    return [
        field
        for step in range(pairs_size)
        for field in (straight[step].at[0], crossed[step // half].at[step % half])
    ]


def assemble(seq_size, pieces, slot, seq_ref, *refs):
    out_any, held_ref, sems = refs[-3:]
    count = sems.shape[0]
    rows, cols, width = held_ref.shape
    rows = rows // count
    tokens = rows * cols

    def source(token):
        row, col = parted(token, cols)
        at, base = 0, jnp.zeros_like(token)
        for piece in pieces:
            inner = piece // seq_size
            local = col - at
            owner, step = parted(local, inner)
            owner = lax.bitwise_xor(owner, seq_ref[0])
            here = (at + owner * inner + step) * rows + row
            base = jnp.where((local >= 0) & (local < piece), here, base)
            at += piece
        return base

    order = permutation(tokens, source)
    copies = []
    for step in range(count):
        own = pl.ds(step * rows, rows)
        gathered = jnp.concatenate(
            [
                field[:, own].reshape(-1, width)
                for at in range(len(pieces))
                for field in in_order(refs, at, seq_size // CORES)
            ],
            axis=0,
        )
        held_ref[own] = dot(order, gathered).astype(BF16).reshape(rows, cols, width)
        copies.append(
            pltpu.make_async_copy(
                held_ref.at[own], out_any.at[own, pl.ds(slot * cols, cols)], sems.at[step]
            )
        )
        copies[-1].start()
    for copy in copies:
        copy.wait()


def params(limit=VMEM_BYTES):
    return pltpu.CompilerParams(vmem_limit_bytes=limit)


def cost(flops, moved, special=0):
    return pl.CostEstimate(flops=int(flops), bytes_accessed=int(moved), transcendentals=int(special))


def on_device(
    states, row_query, row_key, row_value, row_out, col_query, col_key, col_value, col_out
):
    rows, block, width = states.shape
    pairs_size, res_size = lax.axis_size("pair"), HALVES * lax.axis_size("inner")
    seq_size = pairs_size * CORES
    all_rows, cols = rows * seq_size, block * res_size
    head_dim = width // HEADS
    pair = 2 * head_dim
    own_rows = rows // res_size
    half_pairs = HEADS // 2 // CORES
    core = lax.axis_index("core").astype(jnp.int32)
    seq = lax.axis_index("pair").astype(jnp.int32) * CORES + core
    part = lax.axis_index(("half", "inner")).astype(jnp.int32)
    swap = [(0, 1), (1, 0)]
    smem = pl.BlockSpec(memory_space=pltpu.SMEM)
    vmem = pl.BlockSpec(memory_space=pltpu.VMEM)
    anywhere = pl.BlockSpec(memory_space=pl.ANY)
    chunks = [SLOT] * (block // SLOT)

    def across(field, step):
        return lax.ppermute(field, ("half", "inner"), [(at, at ^ step) for at in range(res_size)])

    def around(field, step):
        return lax.ppermute(field, "pair", [(at, at ^ step) for at in range(pairs_size)])

    shares = pl.pallas_call(
        row_shares,
        in_specs=[smem, anywhere],
        out_specs=[anywhere] * (res_size - 1),
        out_shape=[jax.ShapeDtypeStruct((own_rows, block, width), BF16)] * (res_size - 1),
        scratch_shapes=[
            pltpu.VMEM((res_size - 1, own_rows, block, width), BF16),
            pltpu.SemaphoreType.DMA((res_size - 1,)),
            pltpu.SemaphoreType.DMA((res_size - 1,)),
        ],
        compiler_params=params(FULL_VMEM_BYTES),
        name="row_shares",
    )(part.reshape(1), states)
    blocks = {0: states, 1: across(shares[0], 1)}
    for step in range(3, res_size):
        blocks[step] = across(shares[step - 1], step)
    halves = ((1 - core) * half_pairs).reshape(1), (core * half_pairs).reshape(1)
    places = [(part ^ step).reshape(1) for step in range(res_size)]
    own, halves, place, places = lax.optimization_barrier(
        (blocks[0], halves, seq.reshape(1), places)
    )
    blocks[0] = own
    def projected(step, weights, fields, kept):
        count = len(weights) + kept
        return pl.pallas_call(
            functools.partial(row_project, len(weights), kept),
            in_specs=[smem] + [vmem] * (1 + len(weights) + len(fields)),
            out_specs=[vmem] * count,
            out_shape=[jax.ShapeDtypeStruct((own_rows, cols, width), BF16)] * count,
            input_output_aliases={2 + len(weights) + at: at for at in range(len(fields))},
            compiler_params=params(),
            cost_estimate=cost(2 * len(weights) * own_rows * block * width * width, 6e6),
            name="row_project",
        )(places[step], blocks[step], *weights, *fields)

    *early, last = [0, res_size - 1] + list(range(1, res_size - 1))
    fields = []
    for step in early:
        fields = projected(step, [row_query, row_key, row_value], fields, 1)
        if step == 0:
            far, fields = lax.optimization_barrier((shares[1], fields))
            blocks[2] = across(far, 2)
    q, k = projected(last, [row_query, row_key], fields[:2], 0)

    def scores(base):
        return pl.pallas_call(
            functools.partial(row_scores, block, chunks),
            in_specs=[smem, vmem, vmem],
            out_specs=vmem,
            out_shape=jax.ShapeDtypeStruct((half_pairs, cols, 2 * cols), F32),
            compiler_params=params(),
            cost_estimate=cost(4 * own_rows * cols * cols * pair * half_pairs, 2e6),
            name="row_scores",
        )(base, q, k)

    other = lax.ppermute(scores(halves[0]), "core", swap)
    mine = scores(halves[1])
    owners = pairs_size * (res_size // HALVES)
    share = (owners, half_pairs * cols // owners, 2 * cols)
    partial = lax.all_to_all(
        (mine + other).reshape(share), ("pair", "inner"), split_axis=0, concat_axis=0, tiled=True
    )
    partial = pl.pallas_call(
        row_sum,
        in_specs=[vmem],
        out_specs=vmem,
        out_shape=jax.ShapeDtypeStruct(share[1:], F32),
        compiler_params=params(),
        name="row_sum",
    )(partial)
    partial, fields = lax.optimization_barrier((partial, fields[2:]))
    v, x = projected(last, [row_value], fields, 1)
    moved_shape = (len(chunks), own_rows * res_size * SLOT, width)
    kept = pl.pallas_call(
        functools.partial(row_keep, seq_size, res_size),
        in_specs=[vmem],
        out_specs=vmem,
        out_shape=jax.ShapeDtypeStruct(moved_shape, BF16),
        compiler_params=params(),
        cost_estimate=cost(2 * own_rows * cols * width * 512, 3e6),
        name="row_keep",
    )(x)
    prob = pl.pallas_call(
        functools.partial(row_softmax, head_dim ** (-0.5) / math.sqrt(all_rows)),
        in_specs=[vmem, vmem],
        out_specs=vmem,
        out_shape=jax.ShapeDtypeStruct(share, BF16),
        compiler_params=params(),
        name="row_softmax",
    )(partial, lax.ppermute(partial, "half", swap))
    prob, v, kept = lax.optimization_barrier((prob, v, kept))
    prob = lax.all_to_all(prob, ("pair", "inner"), split_axis=0, concat_axis=0, tiled=True)
    prob = prob.reshape(half_pairs, cols, 2 * cols)
    prob_other = lax.ppermute(prob, "core", swap)

    held = pltpu.VMEM((own_rows, cols, width // CORES), BF16)
    attended = pl.pallas_call(
        functools.partial(row_attend, seq_size, res_size),
        in_specs=[smem, vmem, vmem],
        out_specs=vmem,
        out_shape=jax.ShapeDtypeStruct(moved_shape, BF16),
        scratch_shapes=[held],
        compiler_params=params(),
        cost_estimate=cost(2 * own_rows * cols * cols * width, 3e6),
        name="row_attend",
    )(halves[1], prob, v)
    mid, _ = pl.pallas_call(
        functools.partial(row_update, seq_size, res_size),
        in_specs=[smem] + [vmem] * 5,
        out_specs=[vmem, vmem],
        out_shape=[
            jax.ShapeDtypeStruct(
                (seq_size * res_size, block // seq_size, own_rows, width), BF16
            ),
            jax.ShapeDtypeStruct(moved_shape, BF16),
        ],
        scratch_shapes=[held],
        input_output_aliases={5: 1},
        compiler_params=params(),
        cost_estimate=cost(2 * own_rows * cols * width * (width + cols), 8e6),
        name="row_update",
    )(halves[0], prob_other, v, kept, row_out, attended)

    moved = lax.all_to_all(
        mid, ("pair", "core", "half", "inner"), split_axis=0, concat_axis=0, tiled=True
    )
    home = []
    first_at = 0
    for piece in chunks:
        at_once = piece // seq_size
        tokens = at_once * all_rows
        updated = pl.pallas_call(
            functools.partial(column_update, first_at),
            in_specs=[smem] + [vmem] * 5,
            out_shape=[jax.ShapeDtypeStruct((CORES, at_once, rows, width), BF16)] * pairs_size,
            scratch_shapes=[
                pltpu.VMEM((tokens, width), BF16),
                pltpu.VMEM((at_once, all_rows, width), BF16),
            ],
            compiler_params=params(),
            cost_estimate=cost(10 * tokens * width * width, 8e6, tokens * all_rows * HEADS),
            name="column_update",
        )(place, moved, col_query, col_key, col_value, col_out)
        first_at += at_once
        arrived = [updated[0]] + [around(updated[step], step) for step in range(1, pairs_size)]
        crossed = [
            lax.ppermute(jnp.stack([field[1] for field in fields]), "core", swap)
            for fields in (arrived[: pairs_size // 2], arrived[pairs_size // 2 :])
        ]
        home.append(arrived + crossed)

    steps = 2
    out = []
    at = 0
    for slot in range(block // SLOT):
        pieces, parts = [], []
        while sum(pieces) < SLOT:
            pieces.append(chunks[at])
            parts += home[at]
            at += 1
        out = [
            pl.pallas_call(
                functools.partial(assemble, seq_size, pieces, slot),
                in_specs=[smem] + [vmem] * len(parts) + [anywhere] * len(out),
                out_specs=anywhere,
                out_shape=jax.ShapeDtypeStruct((rows, block, width), BF16),
                input_output_aliases={1 + len(parts): 0} if out else {},
                scratch_shapes=[
                    pltpu.VMEM((rows, SLOT, width), BF16),
                    pltpu.SemaphoreType.DMA((steps,)),
                ],
                compiler_params=params(),
                name="assemble",
            )(place, *parts, *out)
        ]
    return out[0]


def solution(mesh):
    seq_size, res_size = mesh.devices.shape
    split = Mesh(
        mesh.devices.reshape(seq_size // CORES, CORES, HALVES, res_size // HALVES),
        ("pair", "core", "half", "inner"),
    )
    placed = P(("pair", "core"), ("half", "inner"), None)
    return jax.shard_map(
        on_device,
        mesh=split,
        in_specs=(placed,) + (P(),) * 8,
        out_specs=placed,
        check_vma=False,
    )
```

```python
import functools
import math

import jax
import jax.numpy as jnp
from jax import lax
from jax.experimental import pallas as pl
from jax.experimental.pallas import tpu as pltpu
from jax.sharding import Mesh
from jax.sharding import PartitionSpec as P

HEADS = 12
CORES = 2
HALVES = 2
SLOT = 16
VMEM_BYTES = 24 * 1024 * 1024
FULL_VMEM_BYTES = 64_000_000

BF16 = jnp.bfloat16
F32 = jnp.float32


def normalize(values):
    center = values - jnp.mean(values, axis=-1, keepdims=True)
    spread = jnp.mean(center * center, axis=-1, keepdims=True)
    return (center * lax.rsqrt(spread + 1e-05)).astype(BF16)


def dot(left, right):
    return jnp.dot(left, right, preferred_element_type=F32)


def dot_nt(left, right):
    return lax.dot_general(left, right, (((1,), (1,)), ((), ())), preferred_element_type=F32)


def head_masks(width, head_dim):
    lane = lax.broadcasted_iota(jnp.int32, (1, width), 1)
    first = (lax.rem(lane, 2 * head_dim) < head_dim).astype(F32)
    return first.astype(BF16), (1.0 - first).astype(BF16)


def permutation(size, source):
    wanted = source(lax.broadcasted_iota(jnp.int32, (size, 1), 0))
    found = lax.broadcasted_iota(jnp.int32, (size, size), 1) == wanted
    return found.astype(F32).astype(BF16)


def parted(number, size):
    return lax.shift_right_logical(number, size.bit_length() - 1), lax.bitwise_and(number, size - 1)


def row_shares(part_ref, states_any, *refs):
    out_refs, (held_ref, in_sems, out_sems) = refs[:-3], refs[-3:]
    rows = held_ref.shape[1]
    arrivals, departures = [], []
    for at, out_ref in enumerate(out_refs):
        owner = lax.bitwise_xor(part_ref[0], at + 1)
        arrivals.append(
            pltpu.make_async_copy(
                states_any.at[pl.ds(owner * rows, rows)], held_ref.at[at], in_sems.at[at]
            )
        )
        departures.append(pltpu.make_async_copy(held_ref.at[at], out_ref, out_sems.at[at]))
    for copy in arrivals:
        copy.start()
    for arrival, departure in zip(arrivals, departures, strict=True):
        arrival.wait()
        departure.start()
    for copy in departures:
        copy.wait()


def row_project(count, kept, at_ref, x_ref, *refs):
    weight_refs, out_refs = refs[:count], refs[len(refs) - count - kept :]
    rows, _, width = out_refs[0].shape
    block = x_ref.shape[1]
    x = x_ref[...] if x_ref.shape[0] == rows else x_ref[pl.ds(at_ref[0] * rows, rows)]
    place = pl.ds(pl.multiple_of(at_ref[0] * block, block), block)
    if kept:
        out_refs[count][:, place, :] = x
    normed = normalize(x.astype(F32).reshape(rows * block, width))
    for weight_ref, ref in zip(weight_refs, out_refs[:count], strict=True):
        ref[:, place, :] = dot(normed, weight_ref[...]).astype(BF16).reshape(rows, block, width)


def row_scores(block, chunks, base_ref, q_ref, k_ref, tied_ref):
    rows, cols, width = q_ref.shape
    pair = 2 * (width // HEADS)
    masks = head_masks(pair, pair // 2)
    for step in range(tied_ref.shape[0]):
        lanes = pl.ds(pl.multiple_of((base_ref[0] + step) * pair, pair), pair)
        q = jnp.concatenate([q_ref[row, :, lanes] for row in range(rows)], axis=1)
        keys = jnp.concatenate(
            [
                jnp.concatenate([k_ref[row, :, lanes] * mask for row in range(rows)], axis=1)
                for mask in masks
            ],
            axis=0,
        )
        score = dot_nt(q, keys).reshape(cols // block, block, 2 * cols)
        at = 0
        pieces = []
        for piece in chunks:
            pieces.append(score[:, at : at + piece].reshape(-1, 2 * cols))
            at += piece
        tied_ref[step] = jnp.concatenate(pieces, axis=0)


def row_sum(parts_ref, tied_ref):
    tied = parts_ref[0]
    for at in range(1, parts_ref.shape[0]):
        tied = tied + parts_ref[at]
    tied_ref[...] = tied


def row_softmax(scale, mine_ref, other_ref, prob_ref):
    tied = (mine_ref[...] + other_ref[...]) * scale
    cols = tied.shape[1] // 2
    halves = []
    for half in (tied[:, :cols], tied[:, cols:]):
        top = jnp.exp(half - jnp.max(half, axis=-1, keepdims=True))
        halves.append(top / jnp.sum(top, axis=-1, keepdims=True))
    prob = jnp.concatenate(halves, axis=1).astype(BF16)
    for at in range(prob_ref.shape[0]):
        prob_ref[at] = prob


def moved_order(rows, parts, piece, inner):
    def source(token):
        rest, row = parted(token, rows)
        rest, step = parted(rest, inner)
        owner, part = parted(rest, parts)
        return (row * parts + part) * piece + owner * inner + step

    return permutation(rows * parts * piece, source)


def row_attend(seq_size, parts, low_ref, prob_ref, v_ref, o_ref, held_ref):
    rows, _, width = v_ref.shape
    pair = 2 * (width // HEADS)
    count = prob_ref.shape[0]
    masks = head_masks(pair, pair // 2)
    for at in range(count):
        lanes = pl.ds(pl.multiple_of((low_ref[0] + at) * pair, pair), pair)
        own = slice(at * pair, (at + 1) * pair)
        prob = prob_ref[at]
        for row in range(0, rows, 2):
            fields = [v_ref[row + step, :, lanes] for step in range(2)]
            values = jnp.concatenate(
                [jnp.concatenate([field * mask for field in fields], axis=1) for mask in masks],
                axis=0,
            )
            result = dot(prob, values).astype(BF16)
            held_ref[row, :, own] = result[:, :pair]
            held_ref[row + 1, :, own] = result[:, pair:]
    lanes = pl.ds(pl.multiple_of(low_ref[0] * pair, pair), count * pair)
    order = moved_order(rows, parts, SLOT, SLOT // seq_size)
    tokens = o_ref.shape[1]
    for chunk in range(o_ref.shape[0]):
        field = held_ref[:, chunk * SLOT * parts : (chunk + 1) * SLOT * parts, :]
        o_ref[chunk, :, lanes] = dot(order, field.reshape(tokens, count * pair)).astype(BF16)


def row_keep(seq_size, parts, x_ref, kept_ref):
    rows, cols, width = x_ref.shape
    order = moved_order(rows, parts, SLOT, SLOT // seq_size)
    for chunk in range(kept_ref.shape[0]):
        field = x_ref[...].reshape(rows, parts, cols // parts, width)
        field = field[:, :, chunk * SLOT : (chunk + 1) * SLOT].reshape(-1, width)
        kept_ref[chunk] = dot(order, field).astype(BF16)


def row_update(seq_size, parts, low_ref, prob_ref, v_ref, kept_ref, wo_ref, _, mid_ref, o_ref, held_ref):
    row_attend(seq_size, parts, low_ref, prob_ref, v_ref, o_ref, held_ref)
    _, _, rows, width = mid_ref.shape
    inner = SLOT // seq_size
    for chunk in range(o_ref.shape[0]):
        mid = kept_ref[chunk].astype(F32) + dot(o_ref[chunk], wo_ref[...])
        own = slice(chunk * inner, (chunk + 1) * inner)
        mid_ref[:, own] = mid.astype(BF16).reshape(-1, inner, rows, width)


def column_update(first_at, seq_ref, mid_ref, wq_ref, wk_ref, wv_ref, wo_ref, *refs):
    out_refs, o_ref, updated_ref = refs[:-2], refs[-2], refs[-1]
    at_once, all_rows, width = updated_ref.shape
    head_dim = width // HEADS
    pair = 2 * head_dim
    scale = head_dim ** (-0.5)

    mid = mid_ref[:, first_at : first_at + at_once].astype(F32)
    mid = jnp.concatenate([mid[:, at].reshape(all_rows, width) for at in range(at_once)], axis=0)
    normed = normalize(mid)
    q = (dot(normed, wq_ref[...]) * scale).astype(BF16)
    k = dot(normed, wk_ref[...]).astype(BF16)
    v = dot(normed, wv_ref[...]).astype(BF16)
    masks = head_masks(pair, head_dim)
    ones = [jnp.broadcast_to(mask, (all_rows, pair)) for mask in masks]

    for at in range(at_once):
        own = slice(at * all_rows, (at + 1) * all_rows)
        for head in range(HEADS // 2):
            lanes = slice(head * pair, (head + 1) * pair)
            keys = jnp.concatenate([k[own, lanes] * mask for mask in masks], axis=0)
            score = dot_nt(q[own, lanes], keys)
            tops = []
            for half in (score[:, :all_rows], score[:, all_rows:]):
                tops.append(jnp.exp(half - jnp.max(half, axis=-1, keepdims=True)).astype(BF16))
            values = jnp.concatenate(
                [
                    jnp.concatenate([v[own, lanes] * mask, one], axis=1)
                    for mask, one in zip(masks, ones, strict=True)
                ],
                axis=0,
            )
            result = dot(jnp.concatenate(tops, axis=1), values)
            o_ref[own, lanes] = (result[:, :pair] / result[:, pair:]).astype(BF16)

    update = dot(o_ref[...], wo_ref[...]).astype(BF16).astype(F32)
    updated_ref[...] = (mid + update).astype(BF16).reshape(at_once, all_rows, width)
    kept = out_refs[0].shape[2]
    for step, out_ref in enumerate(out_refs):
        for other in range(CORES):
            owner = lax.bitwise_xor(seq_ref[0], step * CORES + other)
            out_ref[other] = updated_ref[:, pl.ds(pl.multiple_of(owner * kept, kept), kept), :]


def in_order(refs, at, pairs_size):
    first = at * (pairs_size + 2)
    straight = refs[first : first + pairs_size]
    crossed = refs[first + pairs_size : first + pairs_size + 2]
    half = pairs_size // 2
    return [
        field
        for step in range(pairs_size)
        for field in (straight[step].at[0], crossed[step // half].at[step % half])
    ]


def assemble(seq_size, pieces, slot, seq_ref, *refs):
    out_any, held_ref, sems = refs[-3:]
    count = sems.shape[0]
    rows, cols, width = held_ref.shape
    rows = rows // count
    tokens = rows * cols

    def source(token):
        row, col = parted(token, cols)
        at, base = 0, jnp.zeros_like(token)
        for piece in pieces:
            inner = piece // seq_size
            local = col - at
            owner, step = parted(local, inner)
            owner = lax.bitwise_xor(owner, seq_ref[0])
            here = (at + owner * inner + step) * rows + row
            base = jnp.where((local >= 0) & (local < piece), here, base)
            at += piece
        return base

    order = permutation(tokens, source)
    copies = []
    for step in range(count):
        own = pl.ds(step * rows, rows)
        gathered = jnp.concatenate(
            [
                field[:, own].reshape(-1, width)
                for at in range(len(pieces))
                for field in in_order(refs, at, seq_size // CORES)
            ],
            axis=0,
        )
        held_ref[own] = dot(order, gathered).astype(BF16).reshape(rows, cols, width)
        copies.append(
            pltpu.make_async_copy(
                held_ref.at[own], out_any.at[own, pl.ds(slot * cols, cols)], sems.at[step]
            )
        )
        copies[-1].start()
    for copy in copies:
        copy.wait()


def params(limit=VMEM_BYTES):
    return pltpu.CompilerParams(vmem_limit_bytes=limit)


def cost(flops, moved, special=0):
    return pl.CostEstimate(flops=int(flops), bytes_accessed=int(moved), transcendentals=int(special))


def on_device(
    states, row_query, row_key, row_value, row_out, col_query, col_key, col_value, col_out
):
    rows, block, width = states.shape
    pairs_size, res_size = lax.axis_size("pair"), HALVES * lax.axis_size("inner")
    seq_size = pairs_size * CORES
    all_rows, cols = rows * seq_size, block * res_size
    head_dim = width // HEADS
    pair = 2 * head_dim
    own_rows = rows // res_size
    half_pairs = HEADS // 2 // CORES
    core = lax.axis_index("core").astype(jnp.int32)
    seq = lax.axis_index("pair").astype(jnp.int32) * CORES + core
    part = lax.axis_index(("half", "inner")).astype(jnp.int32)
    swap = [(0, 1), (1, 0)]
    smem = pl.BlockSpec(memory_space=pltpu.SMEM)
    vmem = pl.BlockSpec(memory_space=pltpu.VMEM)
    anywhere = pl.BlockSpec(memory_space=pl.ANY)
    chunks = [SLOT] * (block // SLOT)

    def across(field, step):
        return lax.ppermute(field, ("half", "inner"), [(at, at ^ step) for at in range(res_size)])

    def around(field, step):
        return lax.ppermute(field, "pair", [(at, at ^ step) for at in range(pairs_size)])

    shares = pl.pallas_call(
        row_shares,
        in_specs=[smem, anywhere],
        out_specs=[anywhere] * (res_size - 1),
        out_shape=[jax.ShapeDtypeStruct((own_rows, block, width), BF16)] * (res_size - 1),
        scratch_shapes=[
            pltpu.VMEM((res_size - 1, own_rows, block, width), BF16),
            pltpu.SemaphoreType.DMA((res_size - 1,)),
            pltpu.SemaphoreType.DMA((res_size - 1,)),
        ],
        compiler_params=params(FULL_VMEM_BYTES),
        name="row_shares",
    )(part.reshape(1), states)
    blocks = {0: states, 1: across(shares[0], 1)}
    for step in range(3, res_size):
        blocks[step] = across(shares[step - 1], step)
    halves = ((1 - core) * half_pairs).reshape(1), (core * half_pairs).reshape(1)
    places = [(part ^ step).reshape(1) for step in range(res_size)]
    own, halves, place, places = lax.optimization_barrier(
        (blocks[0], halves, seq.reshape(1), places)
    )
    blocks[0] = own
    def projected(step, weights, fields, kept):
        count = len(weights) + kept
        return pl.pallas_call(
            functools.partial(row_project, len(weights), kept),
            in_specs=[smem] + [vmem] * (1 + len(weights) + len(fields)),
            out_specs=[vmem] * count,
            out_shape=[jax.ShapeDtypeStruct((own_rows, cols, width), BF16)] * count,
            input_output_aliases={2 + len(weights) + at: at for at in range(len(fields))},
            compiler_params=params(),
            cost_estimate=cost(2 * len(weights) * own_rows * block * width * width, 6e6),
            name="row_project",
        )(places[step], blocks[step], *weights, *fields)

    *early, last = [0, res_size - 1] + list(range(1, res_size - 1))
    fields = []
    for step in early:
        fields = projected(step, [row_query, row_key, row_value], fields, 1)
        if step == 0:
            far, fields = lax.optimization_barrier((shares[1], fields))
            blocks[2] = across(far, 2)
    q, k = projected(last, [row_query, row_key], fields[:2], 0)

    def scores(base):
        return pl.pallas_call(
            functools.partial(row_scores, block, chunks),
            in_specs=[smem, vmem, vmem],
            out_specs=vmem,
            out_shape=jax.ShapeDtypeStruct((half_pairs, cols, 2 * cols), F32),
            compiler_params=params(),
            cost_estimate=cost(4 * own_rows * cols * cols * pair * half_pairs, 2e6),
            name="row_scores",
        )(base, q, k)

    other = lax.ppermute(scores(halves[0]), "core", swap)
    mine = scores(halves[1])
    owners = pairs_size * (res_size // HALVES)
    share = (owners, half_pairs * cols // owners, 2 * cols)
    partial = lax.all_to_all(
        (mine + other).reshape(share), ("pair", "inner"), split_axis=0, concat_axis=0, tiled=True
    )
    partial = pl.pallas_call(
        row_sum,
        in_specs=[vmem],
        out_specs=vmem,
        out_shape=jax.ShapeDtypeStruct(share[1:], F32),
        compiler_params=params(),
        name="row_sum",
    )(partial)
    partial, fields = lax.optimization_barrier((partial, fields[2:]))
    v, x = projected(last, [row_value], fields, 1)
    moved_shape = (len(chunks), own_rows * res_size * SLOT, width)
    kept = pl.pallas_call(
        functools.partial(row_keep, seq_size, res_size),
        in_specs=[vmem],
        out_specs=vmem,
        out_shape=jax.ShapeDtypeStruct(moved_shape, BF16),
        compiler_params=params(),
        cost_estimate=cost(2 * own_rows * cols * width * 512, 3e6),
        name="row_keep",
    )(x)
    prob = pl.pallas_call(
        functools.partial(row_softmax, head_dim ** (-0.5) / math.sqrt(all_rows)),
        in_specs=[vmem, vmem],
        out_specs=vmem,
        out_shape=jax.ShapeDtypeStruct(share, BF16),
        compiler_params=params(),
        name="row_softmax",
    )(partial, lax.ppermute(partial, "half", swap))
    prob, v, kept = lax.optimization_barrier((prob, v, kept))
    prob = lax.all_to_all(prob, ("pair", "inner"), split_axis=0, concat_axis=0, tiled=True)
    prob = prob.reshape(half_pairs, cols, 2 * cols)
    prob_other = lax.ppermute(prob, "core", swap)

    held = pltpu.VMEM((own_rows, cols, width // CORES), BF16)
    attended = pl.pallas_call(
        functools.partial(row_attend, seq_size, res_size),
        in_specs=[smem, vmem, vmem],
        out_specs=vmem,
        out_shape=jax.ShapeDtypeStruct(moved_shape, BF16),
        scratch_shapes=[held],
        compiler_params=params(),
        cost_estimate=cost(2 * own_rows * cols * cols * width, 3e6),
        name="row_attend",
    )(halves[1], prob, v)
    mid, _ = pl.pallas_call(
        functools.partial(row_update, seq_size, res_size),
        in_specs=[smem] + [vmem] * 5,
        out_specs=[vmem, vmem],
        out_shape=[
            jax.ShapeDtypeStruct(
                (seq_size * res_size, block // seq_size, own_rows, width), BF16
            ),
            jax.ShapeDtypeStruct(moved_shape, BF16),
        ],
        scratch_shapes=[held],
        input_output_aliases={5: 1},
        compiler_params=params(),
        cost_estimate=cost(2 * own_rows * cols * width * (width + cols), 8e6),
        name="row_update",
    )(halves[0], prob_other, v, kept, row_out, attended)

    moved = lax.all_to_all(
        mid, ("pair", "core", "half", "inner"), split_axis=0, concat_axis=0, tiled=True
    )
    home = []
    first_at = 0
    for piece in chunks:
        at_once = piece // seq_size
        tokens = at_once * all_rows
        updated = pl.pallas_call(
            functools.partial(column_update, first_at),
            in_specs=[smem] + [vmem] * 5,
            out_shape=[jax.ShapeDtypeStruct((CORES, at_once, rows, width), BF16)] * pairs_size,
            scratch_shapes=[
                pltpu.VMEM((tokens, width), BF16),
                pltpu.VMEM((at_once, all_rows, width), BF16),
            ],
            compiler_params=params(),
            cost_estimate=cost(10 * tokens * width * width, 8e6, tokens * all_rows * HEADS),
            name="column_update",
        )(place, moved, col_query, col_key, col_value, col_out)
        first_at += at_once
        arrived = [updated[0]] + [around(updated[step], step) for step in range(1, pairs_size)]
        crossed = [
            lax.ppermute(jnp.stack([field[1] for field in fields]), "core", swap)
            for fields in (arrived[: pairs_size // 2], arrived[pairs_size // 2 :])
        ]
        home.append(arrived + crossed)

    steps = 2
    out = []
    at = 0
    for slot in range(block // SLOT):
        pieces, parts = [], []
        while sum(pieces) < SLOT:
            pieces.append(chunks[at])
            parts += home[at]
            at += 1
        out = [
            pl.pallas_call(
                functools.partial(assemble, seq_size, pieces, slot),
                in_specs=[smem] + [vmem] * len(parts) + [anywhere] * len(out),
                out_specs=anywhere,
                out_shape=jax.ShapeDtypeStruct((rows, block, width), BF16),
                input_output_aliases={1 + len(parts): 0} if out else {},
                scratch_shapes=[
                    pltpu.VMEM((rows, SLOT, width), BF16),
                    pltpu.SemaphoreType.DMA((steps,)),
                ],
                compiler_params=params(),
                name="assemble",
            )(place, *parts, *out)
        ]
    return out[0]


def solution(mesh):
    seq_size, res_size = mesh.devices.shape
    split = Mesh(
        mesh.devices.reshape(seq_size // CORES, CORES, HALVES, res_size // HALVES),
        ("pair", "core", "half", "inner"),
    )
    placed = P(("pair", "core"), ("half", "inner"), None)
    return jax.shard_map(
        on_device,
        mesh=split,
        in_specs=(placed,) + (P(),) * 8,
        out_specs=placed,
        check_vma=False,
    )
```
